512 devices in a mesh: wide: 64 (over y_hi, z, core), narrow: 8 (over x, y_lo).
Axes of the slice: x: 4, y: 4 (y_hi: 2, y_lo: 2; y = y_hi * 2 + y_lo), z: 16, core: 2. Of those that a mesh axis runs over, the one named last changes fastest.
Arguments:
- examples: bfloat16 [320, 8192], P('wide', 'narrow'), may hold values from -6 to 6
- references: bfloat16 [128, 8192], P('wide', 'narrow'), may hold values from -6 to 6
- gate_weight: bfloat16 [8192, 28672], P('narrow', 'wide'), may hold values from -0.0625 to 0.0625
- up_weight: bfloat16 [8192, 28672], P('narrow', 'wide'), may hold values from -0.0625 to 0.0625
- down_weight: bfloat16 [28672, 8192], P('wide', 'narrow'), may hold values from -0.03125 to 0.03125
- cotangent: bfloat16 [320, 8192], P('wide', 'narrow'), may hold values from -6 to 6
- pair_ref: int32 [320, 4], replicated, may hold values from 0 to 127
- points: int32 [8], replicated, may hold values from 1 to 8
Outputs:
- expected: bfloat16 [320, 8192], P('wide', 'narrow')
The draws below stay inside these ranges and needn't reach their ends.
All inputs are finite; a program needn't handle non-finite values.
Results may differ from the reference program's by a relative error of at most 0.005.
Values may be sent and summed in bfloat16 or wider, within the bound.
A program may use at most 64 MiB of HBM per device.

```python
import jax
import jax.numpy as jnp

D = 8192
FF = 28672
REFS = 128
PAIRS = 4
POINTS = 8
EXAMPLES = 320


def touch_ends(drawn, key, smallest, high):
    index_at = [jax.random.randint(jax.random.fold_in(key, axis), (), 0, length) for axis, length in enumerate(drawn.shape)]
    widest = drawn.shape.index(max(drawn.shape))
    next_to = index_at[:widest] + [(index_at[widest] + 1) % drawn.shape[widest]] + index_at[widest + 1:]
    return drawn.at[tuple(index_at)].set(smallest).at[tuple(next_to)].set(high)


def steps_of(own_key, dims, shards, smallest, top_value):
    factor_of = 1.0
    for axis_at, parts in shards:
        heights = jax.random.uniform(jax.random.fold_in(jax.random.fold_in(own_key, 6), axis_at), (parts,), jnp.float32, smallest / len(shards), top_value / len(shards))
        factor_of = factor_of * jnp.repeat(jnp.exp(heights), dims[axis_at] // parts).reshape((-1,) + (1,) * (len(dims) - 1 - axis_at))
    return factor_of


def noise(stream_key, shape, width, bound, cuts=(), dtype=jnp.bfloat16):
    drawn = jax.random.normal(stream_key, shape, jnp.float32) * width
    if len(cuts) > 0:
        drawn = steps_of(stream_key, shape, cuts, -0.22, 0.18) * drawn
    return jnp.clip(drawn, min=-bound, max=bound).astype(dtype)


def setup_inputs(seed: int = 0) -> dict:
    arg_keys = jax.random.split(jax.random.key(seed), 9)
    return {
        "examples": noise(arg_keys[0], (EXAMPLES, D), 1.0, 6.0, ((0, 64), (1, 8))),
        "references": noise(arg_keys[1], (REFS, D), 1.0, 6.0, ((0, 64), (1, 8))),
        "gate_weight": noise(arg_keys[2], (D, FF), D ** -0.5, 0.0625, ((0, 8), (1, 64))),
        "up_weight": noise(arg_keys[3], (D, FF), D ** -0.5, 0.0625, ((0, 8), (1, 64))),
        "down_weight": noise(arg_keys[4], (FF, D), FF ** -0.5, 0.03125, ((0, 64), (1, 8))),
        "cotangent": noise(arg_keys[5], (EXAMPLES, D), 1.0, 6.0, ((0, 64), (1, 8))),
        "pair_ref": touch_ends(jax.random.randint(arg_keys[6], (EXAMPLES, PAIRS), 0, REFS), jax.random.fold_in(arg_keys[6], 1), 0, REFS - 1).astype(jnp.int32),
        "points": touch_ends(jax.random.randint(arg_keys[7], (POINTS,), 1, 9), jax.random.fold_in(arg_keys[7], 1), 1, 8).astype(jnp.int32),
    }


def path_coefficients(example_gate, example_up, reference_gate, reference_up, pair_ref, points):
    alphas = points.astype(jnp.float32) / 8.0
    coef_gate = jnp.zeros(example_gate.shape, jnp.float32)
    coef_up = jnp.zeros(example_gate.shape, jnp.float32)
    for pair_slot in range(pair_ref.shape[1]):
        chosen = pair_ref[:, pair_slot].astype(jnp.int32)
        base_gate = jnp.take(reference_gate, chosen, axis=0)
        base_up = jnp.take(reference_up, chosen, axis=0)
        step_gate = example_gate - base_gate
        step_up = example_up - base_up
        for point_slot in range(alphas.shape[0]):
            position = alphas[point_slot]
            along_gate = base_gate + position * step_gate
            along_up = base_up + position * step_up
            sigmoid = jax.nn.sigmoid(along_gate)
            coef_gate = coef_gate + along_up * sigmoid * (1.0 + along_gate * (1.0 - sigmoid))
            coef_up = coef_up + along_gate * sigmoid
    total = pair_ref.shape[1] * alphas.shape[0]
    return coef_gate / total, coef_up / total


def reference(examples, references, gate_weight, up_weight, down_weight, cotangent, pair_ref, points):
    example_gate = jnp.dot(examples, gate_weight, preferred_element_type=jnp.float32)
    example_up = jnp.dot(examples, up_weight, preferred_element_type=jnp.float32)
    reference_gate = jnp.dot(references, gate_weight, preferred_element_type=jnp.float32)
    reference_up = jnp.dot(references, up_weight, preferred_element_type=jnp.float32)
    upstream = jnp.dot(cotangent, down_weight.T, preferred_element_type=jnp.float32)
    coef_gate, coef_up = path_coefficients(example_gate, example_up, reference_gate, reference_up, pair_ref, points)
    grad_gate = (upstream * coef_gate).astype(jnp.bfloat16)
    grad_up = (upstream * coef_up).astype(jnp.bfloat16)
    result = jnp.dot(grad_gate, gate_weight.T, preferred_element_type=jnp.float32)
    result = result + jnp.dot(grad_up, up_weight.T, preferred_element_type=jnp.float32)
    return result.astype(jnp.bfloat16)
```

```python
import functools

import jax
import jax.numpy as jnp
import numpy as np
from jax import lax
from jax.experimental import pallas as pl
from jax.experimental.pallas import tpu as pltpu
from jax.sharding import Mesh
from jax.sharding import PartitionSpec as P

MESH = pl.DeviceIdType.MESH
BF = jnp.bfloat16
F32 = jnp.float32
Z = 16
NT = (((1,), (1,)), ((), ()))


def dot(a, b):
    return jnp.dot(a, b, preferred_element_type=F32)


def dot_nt(a, b):
    return lax.dot_general(a, b, NT, preferred_element_type=F32)


def slot_offset(p):
    return -((p + 1) // 2) if p % 2 else p // 2


def compact_rows():
    s = np.zeros((48, 64), np.float32)
    for m in range(4):
        for r in range(12):
            s[m * 12 + r, m * 16 + r] = 1
    return s


def chunk_rows():
    s = np.zeros((208, 192), np.float32)
    for q in range(4):
        for h in range(2):
            for c in range(2):
                base = 48 * q + (2 * h + c) * 12
                for i in range(2):
                    s[q * 8 + h * 4 + c * 2 + i, base + 10 + i] = 1
                for i in range(5):
                    s[32 + h * 40 + q * 10 + c * 5 + i, base + i] = 1
                    s[112 + h * 48 + q * 10 + c * 5 + i, base + 5 + i] = 1
    return s


def pack_rows():
    s = np.zeros((384, 320), np.float32)
    for p in range(8):
        for t in range(4):
            for i in range(10):
                s[p * 48 + 10 * t + i, 80 * t + 10 * p + i] = 1
    return s


def row_table():
    t = np.zeros((160, 128), np.int32)
    for r in range(160):
        t[r, 0] = slot_offset(r // 10)
        t[r, 1] = r % 10
    return t


def kernel(
    ex_ref, rf_ref, ct_ref, wg_hbm, wu_hbm, wd_hbm, pair_ref, points_ref,
    sel0_ref, sel_ref, pack_ref, table_ref,
    out_ref,
    wg, wu, wd, wcat, wd2, tile, quad, xbuf, xs, sendb, recvb, onehot, base, accr, acce, accu,
    bdiag, sendc, full, d1send, d1recv, keep, d2send, d2recv, d3send, d3recv, fin, finr,
    wsem, qs, qr, zs, zr, ms, mr, bs, br, cs, cr, d1s, d1r, d2s, d2r, d3s, d3r, fs, fr,
):
    h, z, c = lax.axis_index("h"), lax.axis_index("z"), lax.axis_index("c")
    x, l = lax.axis_index("x"), lax.axis_index("l")
    mine = 2 * x + l
    pending = []

    def send(src, dst, ssem, rsem, dev):
        cp = pltpu.make_async_remote_copy(
            src_ref=src, dst_ref=dst, send_sem=ssem, recv_sem=rsem, device_id=dev, device_id_type=MESH
        )
        cp.start()
        pending.append(cp)
        return cp

    loads = [
        pltpu.make_async_copy(a, b, wsem.at[i])
        for i, (a, b) in enumerate(((wg_hbm, wg), (wu_hbm, wu), (wd_hbm, wd)))
    ]
    for cp in loads:
        cp.start()

    quads = [{"h": lax.rem(h + i // 2, 2), "c": lax.rem(c + i % 2, 2)} for i in range(4)]
    peers = [{"x": lax.rem(x + i // 2, 4), "l": lax.rem(l + i % 2, 2)} for i in range(8)]
    alongz = [{"z": lax.rem(z + slot_offset(p) + Z, Z)} for p in range(Z)]
    barrier = pltpu.get_barrier_semaphore()
    for dev in quads[1:] + peers[1:] + alongz[1:]:
        pl.semaphore_signal(barrier, inc=1, device_id=dev, device_id_type=MESH)

    t = jnp.concatenate(
        [ex_ref[...].astype(F32), ct_ref[...].astype(F32), rf_ref[...].astype(F32), jnp.zeros((4, 1024), F32)], axis=0
    ).astype(BF)
    tile[...] = t
    m = 2 * h + c
    quad[m] = t
    pl.semaphore_wait(barrier, 25)
    qcopies = [send(tile, quad.at[m], qs.at[i], qr.at[i], quads[i]) for i in range(1, 4)]

    for cp in loads:
        cp.wait()

    def prep(a):
        w0 = (0, 0, 128, 256)[a]
        kk = min(256, 448 - w0)
        k = lax.broadcasted_iota(jnp.int32, (kk, 256), 0) + w0
        n = lax.broadcasted_iota(jnp.int32, (kk, 256), 1)
        r = n & 127
        first = 56 * (2 * a + (n >> 7))
        sg = jnp.where((r < 56) & (k == first + r), 1.0, 0.0).astype(BF)
        su = jnp.where((r >= 64) & (r < 120) & (k == first + r - 64), 1.0, 0.0).astype(BF)
        for b in range(4):
            rows = pl.ds(256 * b, 256)
            wcat[rows, pl.ds(256 * a, 256)] = (
                dot(wg[rows, pl.ds(w0, kk)], sg) + dot(wu[rows, pl.ds(w0, kk)], su)
            ).astype(BF)
        k = lax.broadcasted_iota(jnp.int32, (256, kk), 1) + w0
        n = lax.broadcasted_iota(jnp.int32, (256, kk), 0)
        r = n & 63
        sd = jnp.where((r < 56) & (k == 56 * (2 * a + (n >> 7)) + r), 1.0, 0.0).astype(BF)
        for b in range(4):
            cols = pl.ds(256 * b, 256)
            wd2[pl.ds(256 * a, 256), cols] = dot(sd, wd[pl.ds(w0, kk), cols]).astype(BF)

    prep(0)

    for cp in qcopies:
        cp.wait_recv()
    xbuf[0] = dot(sel0_ref[...], quad[...].reshape(64, 1024)).astype(BF)

    onward = {"z": lax.rem(z + 1 - 2 * c + Z, Z)}
    mate = {"c": 1 - c}

    def own_slot(s):
        return 2 * s - 1 + (c if s < 8 else 0)

    def columns(s, u):
        return pl.ds(pl.multiple_of((512 * c) if s == 8 else 512 * u, 512), 512)

    def zcopy(s, u):
        src = xbuf.at[0 if s == 1 else own_slot(s - 1), :, columns(s, u)]
        return send(src, xbuf.at[own_slot(s), :, columns(s, u)], zs.at[2 * s + u], zr.at[2 * s + u], onward)

    def mcopy(s, u):
        at = xbuf.at[own_slot(s), :, columns(s, u)]
        return send(at, at, ms.at[2 * s + u], mr.at[2 * s + u], mate)

    def work(k):
        xs[...] = dot(sel_ref[...], xbuf[4 * k : 4 * k + 4].reshape(192, 1024)).astype(BF)
        left = lax.broadcasted_iota(jnp.int32, (48, 256), 1) & 127

        @pl.loop(0, 4)
        def _(n):
            cols = pl.ds(pl.multiple_of(256 * n, 256), 256)
            p = dot(xs[0:112], wcat[:, cols]).astype(BF)
            d = dot_nt(xs[112:208], wd2[cols, :])
            d = jnp.where(left < 64, d[:48], d[48:]).astype(BF)
            for e in range(2):
                sendb[k, 2 * n + e, 0:112] = p[:, 128 * e : 128 * e + 128]
                sendb[k, 2 * n + e, 112:160] = d[:, 128 * e : 128 * e + 128]

        for i in range(1, 8):
            j = 2 * lax.rem(x + i // 2, 4) + lax.rem(l + i % 2, 2)
            bcopies[k, i] = send(sendb.at[k, j], recvb.at[k, i], bs.at[8 * k + i], br.at[8 * k + i], peers[i])

    bcopies, done = {}, {}
    zc = {(1, u): zcopy(1, u) for u in range(2)}
    mc = {}

    def choose():
        off, place = table_ref[:, 0:1], table_ref[:, 1:2]
        want = ((z + off + Z) & (Z - 1)) * 10 + place
        perm = jnp.where(lax.broadcasted_iota(jnp.int32, (160, 160), 1) == want, 1.0, 0.0).astype(BF)
        for hh in range(2):
            rows = pair_ref[160 * hh : 160 * hh + 160, :].astype(F32).astype(BF)
            r = dot(perm, rows).astype(jnp.int32)
            delta = (((r >> 2) & 15) - z + Z) & (Z - 1)
            slot = jnp.where(delta < 8, 2 * delta, 2 * (Z - delta) - 1)
            pos = slot * 8 + (r >> 6) * 4 + (r & 3)
            lane = lax.broadcasted_iota(jnp.int32, (160, 128), 1)
            for p in range(4):
                onehot[p, :, 128 * hh : 128 * hh + 128] = jnp.where(lane == pos[:, p : p + 1], 1.0, 0.0).astype(BF)

    for s in range(1, 9):
        for u in range(2 if s < 8 else 1):
            zc[s, u].wait_recv()
            if s < 7 or (s == 7 and u == 1):
                for v in ([u] if s < 7 else [0]):
                    zc[s + 1, v] = zcopy(s + 1, v)
            mc[s, u] = mcopy(s, u)
        if s < 4:
            prep(s)
        if s == 4:
            choose()
        if s >= 4:
            k = s - 4
            if k < 3:
                pass
        if s in (4, 6, 7):
            k = {4: 0, 6: 1, 7: 2}[s]
            for q in range(1, 2 * k + 3):
                for u in range(2):
                    if not done.get((q, u)):
                        done[q, u] = True
                        mc[q, u].wait_recv()
            work(k)
    for q in range(1, 9):
        for u in range(2 if q < 8 else 1):
            if not done.get((q, u)):
                done[q, u] = True
                mc[q, u].wait_recv()
    work(3)

    lane = lax.broadcasted_iota(jnp.int32, (160, 128), 1)
    for k in range(4):
        total = sendb[k, mine].astype(F32)
        for i in range(1, 8):
            bcopies[k, i].wait_recv()
            total = total + recvb[k, i].astype(F32)
        accr[32 * k : 32 * k + 32] = total[0:32]
        e0, e1 = total[32:72], total[72:112]
        half = lane[:40] < 64
        acce[0, 40 * k : 40 * k + 40] = jnp.where(half, e0, pltpu.roll(e1, 64, 1))
        acce[1, 40 * k : 40 * k + 40] = jnp.where(half, pltpu.roll(e0, 64, 1), e1)
        accu[40 * k : 40 * k + 40] = total[112:152]

    refs = accr[...]
    turned = pltpu.roll(refs, 64, 1)
    left = lane[:128] < 64
    diag = (
        jnp.where(left, refs, 0.0), jnp.where(left, 0.0, turned),
        jnp.where(left, turned, 0.0), jnp.where(left, 0.0, refs),
    )
    for n, block in enumerate(diag):
        high = block.astype(BF)
        low = (block - high.astype(F32)).astype(BF)
        at = (slice(128 * (n % 2), 128 * (n % 2) + 128), slice(128 * (n // 2), 128 * (n // 2) + 128))
        bdiag[(0, *at)] = high
        bdiag[(1, *at)] = low
    for p in range(4):
        base[p] = dot(onehot[p], bdiag[0]) + dot(onehot[p], bdiag[1])

    alphas = [points_ref[i].astype(F32) * 0.125 for i in range(8)]

    @pl.loop(0, 5)
    def _(n):
        rows = pl.ds(pl.multiple_of(32 * n, 32), 32)
        eg, eu, up = acce[0, rows], acce[1, rows], accu[rows]
        cg = jnp.zeros((32, 128), F32)
        cu = jnp.zeros((32, 128), F32)
        for p in range(4):
            bg, bu = base[p, rows, 0:128], base[p, rows, 128:256]
            dg, du = eg - bg, eu - bu
            for a in alphas:
                g = bg + a * dg
                u = bu + a * du
                s = 0.5 * jnp.tanh(0.5 * g) + 0.5
                gs = g * s
                cu = cu + gs
                cg = cg + u * (s + gs * (1.0 - s))
        cg = up * (cg * (1.0 / 32.0))
        cu = up * (cu * (1.0 / 32.0))
        half = lax.broadcasted_iota(jnp.int32, (32, 128), 1) < 64
        sendc[rows, :] = jnp.where(half, cg, pltpu.roll(cu, 64, 1)).astype(BF)
        sendc[pl.ds(pl.multiple_of(160 + 32 * n, 32), 32), :] = jnp.where(half, pltpu.roll(cg, 64, 1), cu).astype(BF)

    lanes = pl.ds(pl.multiple_of(128 * mine, 128), 128)
    ccopies = [send(sendc, full.at[:, lanes], cs.at[i], cr.at[i], peers[i]) for i in range(1, 8)]
    full[:, lanes] = sendc[...]
    for cp in ccopies:
        cp.wait_recv()

    def product(hh, cc, into, at):
        rows = pl.ds(pl.multiple_of(160 * hh, 160), 160)

        @pl.loop(0, 2)
        def _(n):
            w = pl.ds(pl.multiple_of(512 * cc + 256 * n, 256), 256)
            into[at, :, pl.ds(pl.multiple_of(256 * n, 256), 256)] = dot_nt(full[rows, :], wcat[w, :])

    d1 = []
    product(1 - h, 1 - c, d1send, 0)
    d1.append(send(d1send.at[0], d1recv.at[0], d1s.at[0], d1r.at[0], mate))
    product(1 - h, c, keep, 0)
    d1[0].wait_recv()
    d2send[...] = (keep[0] + d1recv[0]).astype(BF)
    d2 = send(d2send, d2recv, d2s, d2r, {"h": 1 - h})
    product(h, 1 - c, d1send, 1)
    d1.append(send(d1send.at[1], d1recv.at[1], d1s.at[1], d1r.at[1], mate))
    product(h, c, keep, 1)
    d1[1].wait_recv()
    keep[1] = keep[1] + d1recv[1]
    d2.wait_recv()
    d3 = []
    for g in range(2):
        rows = slice(80 * g, 80 * g + 80)
        v = (keep[1, rows] + d2recv[rows].astype(F32)).astype(BF)
        v = jnp.concatenate([v[:, 128 * t : 128 * t + 128] for t in range(4)], axis=0)
        d3send[8 * g : 8 * g + 8] = dot(pack_ref[...], v).astype(BF).reshape(8, 48, 128)
        for p in range(8 * g, 8 * g + 8):
            if p:
                d3.append(send(d3send.at[p], d3recv.at[p], d3s.at[p], d3r.at[p], alongz[p]))
    total = d3send[0].astype(F32)
    for p in range(1, Z):
        d3[p - 1].wait_recv()
        total = total + d3recv[p].astype(F32)
    fin[...] = total
    last = send(fin, finr, fs, fr, mate)
    last.wait_recv()
    other = finr[...]
    first = c == 0
    parts = []
    for block in (jnp.where(first, total, other), jnp.where(first, other, total)):
        for t in range(4):
            parts.append(jnp.where(first, block[10 * t : 10 * t + 5], block[10 * t + 5 : 10 * t + 10]))
    out_ref[...] = jnp.concatenate(parts, axis=1).astype(BF)
    for cp in pending:
        cp.wait_send()


def on_device(examples, references, gate_weight, up_weight, down_weight, cotangent, pair_ref, points):
    vm = pl.BlockSpec(memory_space=pltpu.VMEM)
    hbm = pl.BlockSpec(memory_space=pl.ANY)
    sm = pl.BlockSpec(memory_space=pltpu.SMEM)
    dma = pltpu.SemaphoreType.DMA
    V = pltpu.VMEM
    return pl.pallas_call(
        kernel,
        out_shape=jax.ShapeDtypeStruct((5, 1024), BF),
        in_specs=[vm, vm, vm, hbm, hbm, hbm, vm, sm, vm, vm, vm, vm],
        out_specs=vm,
        scratch_shapes=[
            V((1024, 448), BF), V((1024, 448), BF), V((448, 1024), BF),
            V((1024, 1024), BF), V((1024, 1024), BF),
            V((16, 1024), BF), V((4, 16, 1024), BF), V((Z, 48, 1024), BF), V((208, 1024), BF),
            V((4, 8, 160, 128), BF), V((4, 8, 160, 128), BF),
            V((4, 160, 256), BF), V((4, 160, 256), F32),
            V((128, 128), F32), V((2, 160, 128), F32), V((160, 128), F32),
            V((2, 256, 256), BF), V((320, 128), BF), V((320, 1024), BF),
            V((2, 160, 512), F32), V((2, 160, 512), F32), V((2, 160, 512), F32),
            V((160, 512), BF), V((160, 512), BF),
            V((Z, 48, 128), BF), V((Z, 48, 128), BF), V((48, 128), F32), V((48, 128), F32),
            dma((3,)), dma((4,)), dma((4,)), dma((18,)), dma((18,)), dma((18,)), dma((18,)),
            dma((32,)), dma((32,)), dma((8,)), dma((8,)), dma((2,)), dma((2,)), dma, dma,
            dma((Z,)), dma((Z,)), dma, dma,
        ],
        compiler_params=pltpu.CompilerParams(
            collective_id=0, has_side_effects=True, vmem_limit_bytes=48 * 1024 * 1024
        ),
        cost_estimate=pl.CostEstimate(flops=2 * 10**9, bytes_accessed=4 * 10**6, transcendentals=10**6),
    )(
        examples, references, cotangent, gate_weight, up_weight, down_weight, pair_ref, points,
        jnp.asarray(compact_rows(), BF), jnp.asarray(chunk_rows(), BF),
        jnp.asarray(pack_rows(), BF), jnp.asarray(row_table()),
    )


def solution(mesh):
    split = Mesh(mesh.devices.reshape(2, Z, 2, 4, 2), ("h", "z", "c", "x", "l"))
    wide, narrow = ("h", "z", "c"), ("x", "l")
    return jax.shard_map(
        on_device,
        mesh=split,
        in_specs=(
            P(wide, narrow), P(wide, narrow), P(narrow, wide), P(narrow, wide),
            P(wide, narrow), P(wide, narrow), P(), P(),
        ),
        out_specs=P(wide, narrow),
        check_vma=False,
    )
```

```python
import functools

import jax
import jax.numpy as jnp
import numpy as np
from jax import lax
from jax.experimental import pallas as pl
from jax.experimental.pallas import tpu as pltpu
from jax.sharding import Mesh
from jax.sharding import PartitionSpec as P

MESH = pl.DeviceIdType.MESH
BF = jnp.bfloat16
F32 = jnp.float32
Z = 16
NT = (((1,), (1,)), ((), ()))


def dot(a, b):
    return jnp.dot(a, b, preferred_element_type=F32)


def dot_nt(a, b):
    return lax.dot_general(a, b, NT, preferred_element_type=F32)


OFFSETS = (0, 1, -1, 2, -2, 4, -4, 8, 3, -3, 5, -5, 6, -6, 7, -7)


def slot_of(offset):
    return next(p for p in range(Z) if (OFFSETS[p] - offset) % Z == 0)


def compact_rows():
    s = np.zeros((48, 64), np.float32)
    for m in range(4):
        for r in range(12):
            s[m * 12 + r, m * 16 + r] = 1
    return s


def chunk_rows():
    s = np.zeros((4, 208, 768), np.float32)
    for t in range(4):
        for q in range(4):
            for h in range(2):
                for c in range(2):
                    base = 48 * (4 * (2 * h + c) + q) + 12 * t
                    for i in range(2):
                        s[t, q * 8 + h * 4 + c * 2 + i, base + 10 + i] = 1
                    for i in range(5):
                        s[t, 32 + h * 40 + q * 10 + c * 5 + i, base + i] = 1
                        s[t, 112 + h * 48 + q * 10 + c * 5 + i, base + 5 + i] = 1
    return s


def pack_rows():
    s = np.zeros((384, 320), np.float32)
    for p in range(8):
        for t in range(4):
            for i in range(10):
                s[p * 48 + 10 * t + i, 80 * t + 10 * p + i] = 1
    return s


def row_table():
    t = np.zeros((160, 128), np.int32)
    for r in range(160):
        t[r, 0] = OFFSETS[r // 10]
        t[r, 1] = r % 10
    return t


def kernel(
    ex_ref, rf_ref, ct_ref, wg_hbm, wu_hbm, wd_hbm, pair_ref, points_ref,
    sel0_ref, sel_hbm, pack_hbm, table_ref,
    out_ref,
    wg, wu, wd, sel, pack, wcat, wd2, xbuf, xs, sendb, recvb, keepb, lsend, lrecv, onehot, base, accr, acce, accu,
    bdiag, sendc, full, d1send, d1recv, keep, d2send, d2recv, d3send, d3recv, fin, finr,
    wsem, zs, zr, hs, hr, ms, mr, gs, gr, bs, br, ls, lr, cs, cr, d1s, d1r, d2s, d2r, d3s, d3r, fs, fr,
):
    h, z, c = lax.axis_index("h"), lax.axis_index("z"), lax.axis_index("c")
    x, l = lax.axis_index("x"), lax.axis_index("l")
    mine = 2 * x + l
    m, mh = 2 * h + c, 2 * (1 - h) + c
    pending = []

    def send(src, dst, ssem, rsem, dev):
        cp = pltpu.make_async_remote_copy(
            src_ref=src, dst_ref=dst, send_sem=ssem, recv_sem=rsem, device_id=dev, device_id_type=MESH
        )
        cp.start()
        pending.append(cp)
        return cp

    def along(offset):
        return {"z": lax.rem(z + offset + Z, Z)}

    facing, mate, beside = {"h": 1 - h}, {"c": 1 - c}, {"l": 1 - l}
    row = [{"x": lax.rem(x + i, 4)} for i in range(4)]
    peers = [{"x": lax.rem(x + i // 2, 4), "l": lax.rem(l + i % 2, 2)} for i in range(8)]
    barrier = pltpu.get_barrier_semaphore()
    for dev in [along(e) for e in (8, 4, -4, 2, -2, 1, -1)] + [facing] + row[1:] + [beside, mate]:
        pl.semaphore_signal(barrier, inc=1, device_id=dev, device_id_type=MESH)

    loads = [
        pltpu.make_async_copy(a, b, wsem.at[i])
        for i, (a, b) in enumerate(((wg_hbm, wg), (wu_hbm, wu), (wd_hbm, wd), (sel_hbm, sel), (pack_hbm, pack)))
    ]
    for cp in loads:
        cp.start()

    t = jnp.concatenate(
        [ex_ref[...].astype(F32), ct_ref[...].astype(F32), rf_ref[...].astype(F32), jnp.zeros((4, 1024), F32)], axis=0
    ).astype(BF)
    t = jnp.concatenate([t[:, 256 * i : 256 * i + 256] for i in range(4)], axis=0)
    xbuf[0, m, 0] = dot(sel0_ref[...], t).astype(BF)
    pl.semaphore_wait(barrier, 13)

    def block(p):
        return xbuf.at[p // 4, m, p % 4]

    zc = {}

    def zsend(offset, e):
        p = slot_of(offset - e)
        zc[p] = send(block(slot_of(offset)), block(p), zs.at[p], zr.at[p], along(e))

    for e in (8, 4, -4, 2, -2, 1, -1):
        zsend(0, e)

    for cp in loads:
        cp.wait()

    def prep(a):
        w0 = (0, 0, 128, 256)[a]
        kk = min(256, 448 - w0)
        k = lax.broadcasted_iota(jnp.int32, (256, kk), 1) + w0
        n = lax.broadcasted_iota(jnp.int32, (256, kk), 0)
        r = n & 127
        first = 56 * (2 * a + (n >> 7))
        gate = (r < 56) & (k == first + r)
        up = (r >= 64) & (r < 120) & (k == first + r - 64)
        sg = jnp.where(gate, 1.0, 0.0).astype(BF)
        su = jnp.where(up, 1.0, 0.0).astype(BF)
        sd = jnp.where(gate | up, 1.0, 0.0).astype(BF)
        for b in range(4):
            cols = pl.ds(256 * b, 256)
            rows = pl.ds(w0, kk)
            wcat[pl.ds(256 * a, 256), cols] = (dot(sg, wg[rows, cols]) + dot(su, wu[rows, cols])).astype(BF)
            wd2[pl.ds(256 * a, 256), cols] = dot(sd, wd[rows, cols]).astype(BF)

    hc, mc, gc = {}, {}, {}

    def spread(k):
        for q in range(4):
            if 4 * k + q and 4 * k + q not in (5, 6, 7):
                zc[4 * k + q].wait_recv()
        at = xbuf.at[k, m]
        hc[k] = send(at, at, hs.at[k], hr.at[k], facing)
        mc[k] = send(at, at, ms.at[k], mr.at[k], mate)

    def onward(k):
        hc[k].wait_recv()
        at = xbuf.at[k, mh]
        gc[k] = send(at, at, gs.at[k], gr.at[k], mate)

    def work(k):
        mc[k].wait_recv()
        gc[k].wait_recv()
        blocks = xbuf[k].reshape(768, 256)
        for i in range(4):
            xs[:, 256 * i : 256 * i + 256] = dot(sel[i], blocks).astype(BF)
        left = lax.broadcasted_iota(jnp.int32, (48, 256), 1) & 127

        @pl.loop(0, 4)
        def _(n):
            cols = pl.ds(pl.multiple_of(256 * n, 256), 256)
            p = dot_nt(xs[0:112], wcat[cols, :]).astype(BF)
            d = dot_nt(xs[112:208], wd2[cols, :])
            d = jnp.where(left < 64, d[:48], d[48:]).astype(BF)
            for e in range(2):
                sendb[k, n, e, 0:112] = p[:, 128 * e : 128 * e + 128]
                sendb[k, n, e, 112:160] = d[:, 128 * e : 128 * e + 128]

        for i in range(1, 4):
            bc[k, i] = send(
                sendb.at[k, lax.rem(x + i, 4)], recvb.at[k, i], bs.at[4 * k + i], br.at[4 * k + i], row[i]
            )

    bc, lc = {}, {}

    def owner_sum(k):
        for i in range(1, 4):
            bc[k, i].wait_recv()
        theirs = sendb[k, x, 1 - l].astype(F32)
        for i in range(1, 4):
            theirs = theirs + recvb[k, i, 1 - l].astype(F32)
        lsend[k] = theirs
        lc[k] = send(lsend.at[k], lrecv.at[k], ls.at[k], lr.at[k], beside)
        ours = sendb[k, x, l].astype(F32)
        for i in range(1, 4):
            ours = ours + recvb[k, i, l].astype(F32)
        keepb[k] = ours

    def owner_end(k):
        lc[k].wait_recv()
        total = keepb[k] + lrecv[k]
        accr[32 * k : 32 * k + 32] = total[0:32]
        e0, e1 = total[32:72], total[72:112]
        half = lax.broadcasted_iota(jnp.int32, (40, 128), 1) < 64
        acce[0, 40 * k : 40 * k + 40] = jnp.where(half, e0, pltpu.roll(e1, 64, 1))
        acce[1, 40 * k : 40 * k + 40] = jnp.where(half, pltpu.roll(e0, 64, 1), e1)
        accu[40 * k : 40 * k + 40] = total[112:152]

    def choose():
        off, place = table_ref[:, 0:1], table_ref[:, 1:2]
        want = ((z + off + Z) & (Z - 1)) * 10 + place
        perm = jnp.where(lax.broadcasted_iota(jnp.int32, (160, 160), 1) == want, 1.0, 0.0).astype(BF)
        for hh in range(2):
            picks = pair_ref[...].astype(F32)[:, 160 * hh : 160 * hh + 160].astype(BF)
            r = dot_nt(perm, picks).astype(jnp.int32)
            delta = (((r >> 2) & 15) - z + Z) & (Z - 1)
            slot = jnp.zeros_like(delta)
            for p in range(1, Z):
                slot = jnp.where(delta == OFFSETS[p] % Z, p, slot)
            pos = slot * 8 + (r >> 6) * 4 + (r & 3)
            lane = lax.broadcasted_iota(jnp.int32, (160, 128), 1)
            for p in range(4):
                onehot[p, :, 128 * hh : 128 * hh + 128] = jnp.where(lane == pos[:, p : p + 1], 1.0, 0.0).astype(BF)

    prep(0)
    prep(1)
    for p in (7, 5, 6):
        zc[p].wait_recv()
        for offset, e in {7: ((8, 1), (8, -1)), 5: ((4, -2), (4, 1), (4, -1)), 6: ((-4, 2), (-4, 1), (-4, -1))}[p]:
            zsend(offset, e)
    spread(0)
    spread(1)
    prep(2)
    prep(3)
    onward(0)
    onward(1)
    work(0)
    spread(2)
    work(1)
    spread(3)
    choose()
    onward(2)
    owner_sum(0)
    work(2)
    onward(3)
    owner_sum(1)
    work(3)
    owner_end(0)
    owner_sum(2)
    owner_end(1)
    owner_sum(3)
    owner_end(2)
    owner_end(3)

    lane = lax.broadcasted_iota(jnp.int32, (160, 128), 1)
    refs = accr[...]
    turned = pltpu.roll(refs, 64, 1)
    left = lane[:128] < 64
    diag = (
        jnp.where(left, refs, 0.0), jnp.where(left, 0.0, turned),
        jnp.where(left, turned, 0.0), jnp.where(left, 0.0, refs),
    )
    for n, block in enumerate(diag):
        high = block.astype(BF)
        low = (block - high.astype(F32)).astype(BF)
        at = (slice(128 * (n % 2), 128 * (n % 2) + 128), slice(128 * (n // 2), 128 * (n // 2) + 128))
        bdiag[(0, *at)] = high
        bdiag[(1, *at)] = low
    for p in range(4):
        base[p] = dot(onehot[p], bdiag[0]) + dot(onehot[p], bdiag[1])

    alphas = [points_ref[i].astype(F32) * 0.125 for i in range(8)]

    lanes = pl.ds(pl.multiple_of(128 * mine, 128), 128)
    cc = {}

    def coefs(part):
        @pl.loop(0, 5)
        def _(n):
            rows = pl.ds(pl.multiple_of(80 * part + 16 * n, 16), 16)
            eg, eu, up = acce[0, rows], acce[1, rows], accu[rows]
            cg = jnp.zeros((16, 128), F32)
            cu = jnp.zeros((16, 128), F32)
            for p in range(4):
                bg, bu = base[p, rows, 0:128], base[p, rows, 128:256]
                dg, du = eg - bg, eu - bu
                for a in alphas:
                    g = bg + a * dg
                    u = bu + a * du
                    s = 0.5 * jnp.tanh(0.5 * g) + 0.5
                    gs = g * s
                    cu = cu + gs
                    cg = cg + u * (s + gs * (1.0 - s))
            cg = up * (cg * (1.0 / 32.0))
            cu = up * (cu * (1.0 / 32.0))
            half = lax.broadcasted_iota(jnp.int32, (16, 128), 1) < 64
            first = pl.ds(pl.multiple_of(16 * n, 16), 16)
            second = pl.ds(pl.multiple_of(80 + 16 * n, 16), 16)
            sendc[part, first, :] = jnp.where(half, cg, pltpu.roll(cu, 64, 1)).astype(BF)
            sendc[part, second, :] = jnp.where(half, pltpu.roll(cg, 64, 1), cu).astype(BF)

        for i in range(1, 8):
            n = 8 * part + i
            cc[part, i] = send(sendc.at[part], full.at[part, :, lanes], cs.at[n], cr.at[n], peers[i])
        full[part, :, lanes] = sendc[part]

    def product(part, hh, col, into, at):
        rows = pl.ds(pl.multiple_of(80 * hh, 16), 80)

        @pl.loop(0, 2)
        def _(n):
            w = pl.ds(pl.multiple_of(512 * col + 256 * n, 256), 256)
            into[at, :, pl.ds(pl.multiple_of(256 * n, 256), 256)] = dot(full[part, rows, :], wcat[:, w])

    d1, d2, d3 = {}, {}, {}

    def products(part):
        for i in range(1, 8):
            cc[part, i].wait_recv()
        for i, hh in enumerate((1 - h, h)):
            at = 2 * part + i
            product(part, hh, 1 - c, d1send, at)
            d1[at] = send(d1send.at[at], d1recv.at[at], d1s.at[at], d1r.at[at], mate)
            product(part, hh, c, keep, at)
        d1[2 * part].wait_recv()
        d2send[part] = (keep[2 * part] + d1recv[2 * part]).astype(BF)
        d2[part] = send(d2send.at[part], d2recv.at[part], d2s.at[part], d2r.at[part], facing)

    def scatter(part):
        d1[2 * part + 1].wait_recv()
        v = keep[2 * part + 1] + d1recv[2 * part + 1]
        d2[part].wait_recv()
        v = (v + d2recv[part].astype(F32)).astype(BF)
        v = jnp.concatenate([v[:, 128 * t : 128 * t + 128] for t in range(4)], axis=0)
        d3send[8 * part : 8 * part + 8] = dot(pack[...], v).astype(BF).reshape(8, 48, 128)
        for p in range(8 * part, 8 * part + 8):
            if p:
                d3[p] = send(d3send.at[p], d3recv.at[p], d3s.at[p], d3r.at[p], along(OFFSETS[p]))

    coefs(0)
    coefs(1)
    products(0)
    products(1)
    scatter(0)
    scatter(1)
    total = d3send[0].astype(F32)
    for p in range(1, Z):
        d3[p].wait_recv()
        total = total + d3recv[p].astype(F32)
    fin[...] = total
    last = send(fin, finr, fs, fr, mate)
    last.wait_recv()
    other = finr[...]
    first = c == 0
    parts = []
    for block in (jnp.where(first, total, other), jnp.where(first, other, total)):
        for t in range(4):
            parts.append(jnp.where(first, block[10 * t : 10 * t + 5], block[10 * t + 5 : 10 * t + 10]))
    out_ref[...] = jnp.concatenate(parts, axis=1).astype(BF)
    for cp in pending:
        cp.wait_send()


def on_device(examples, references, gate_weight, up_weight, down_weight, cotangent, pair_ref, points):
    vm = pl.BlockSpec(memory_space=pltpu.VMEM)
    hbm = pl.BlockSpec(memory_space=pltpu.HBM)
    sm = pl.BlockSpec(memory_space=pltpu.SMEM)
    dma = pltpu.SemaphoreType.DMA
    V = pltpu.VMEM
    return pl.pallas_call(
        kernel,
        out_shape=jax.ShapeDtypeStruct((5, 1024), BF),
        in_specs=[vm, vm, vm, hbm, hbm, hbm, vm, sm, vm, hbm, hbm, vm],
        out_specs=vm,
        scratch_shapes=[
            V((448, 1024), BF), V((448, 1024), BF), V((448, 1024), BF), V((4, 208, 768), BF), V((384, 320), BF),
            V((1024, 1024), BF), V((1024, 1024), BF),
            V((4, 4, 4, 48, 256), BF), V((208, 1024), BF),
            V((4, 4, 2, 160, 128), BF), V((4, 4, 2, 160, 128), BF),
            V((4, 160, 128), F32), V((4, 160, 128), F32), V((4, 160, 128), F32),
            V((4, 160, 256), BF), V((4, 160, 256), F32),
            V((128, 128), F32), V((2, 160, 128), F32), V((160, 128), F32),
            V((2, 256, 256), BF), V((2, 160, 128), BF), V((2, 160, 1024), BF),
            V((4, 80, 512), F32), V((4, 80, 512), F32), V((4, 80, 512), F32),
            V((2, 80, 512), BF), V((2, 80, 512), BF),
            V((Z, 48, 128), BF), V((Z, 48, 128), BF), V((48, 128), F32), V((48, 128), F32),
            dma((5,)), dma((Z,)), dma((Z,)), dma((4,)), dma((4,)), dma((4,)), dma((4,)), dma((4,)), dma((4,)),
            dma((16,)), dma((16,)), dma((4,)), dma((4,)), dma((16,)), dma((16,)), dma((4,)), dma((4,)),
            dma((2,)), dma((2,)), dma((Z,)), dma((Z,)), dma, dma,
        ],
        compiler_params=pltpu.CompilerParams(
            collective_id=0, has_side_effects=True, vmem_limit_bytes=60 * 1024 * 1024
        ),
        cost_estimate=pl.CostEstimate(flops=2 * 10**9, bytes_accessed=4 * 10**6, transcendentals=10**6),
    )(
        examples, references, cotangent, gate_weight.T, up_weight.T, down_weight, pair_ref.T, points,
        jnp.asarray(compact_rows(), BF), jnp.asarray(chunk_rows(), BF),
        jnp.asarray(pack_rows(), BF), jnp.asarray(row_table()),
    )


def solution(mesh):
    split = Mesh(mesh.devices.reshape(2, Z, 2, 4, 2), ("h", "z", "c", "x", "l"))
    wide, narrow = ("h", "z", "c"), ("x", "l")
    return jax.shard_map(
        on_device,
        mesh=split,
        in_specs=(
            P(wide, narrow), P(wide, narrow), P(narrow, wide), P(narrow, wide),
            P(wide, narrow), P(wide, narrow), P(), P(),
        ),
        out_specs=P(wide, narrow),
        check_vma=False,
    )
```

```python
import functools

import jax
import jax.numpy as jnp
import numpy as np
from jax import lax
from jax.experimental import pallas as pl
from jax.experimental.pallas import tpu as pltpu
from jax.sharding import Mesh
from jax.sharding import PartitionSpec as P

MESH = pl.DeviceIdType.MESH
BF = jnp.bfloat16
F32 = jnp.float32
Z = 16
NT = (((1,), (1,)), ((), ()))


def dot(a, b):
    return jnp.dot(a, b, preferred_element_type=F32)


def dot_nt(a, b):
    return lax.dot_general(a, b, NT, preferred_element_type=F32)


OFFSETS = (0, 1, -1, 2, -2, 4, -4, 8, 3, -3, 5, -5, 6, -6, 7, -7)


def slot_of(offset):
    return next(p for p in range(Z) if (OFFSETS[p] - offset) % Z == 0)


def compact_rows():
    s = np.zeros((96, 128), np.float32)
    for t in range(8):
        for r in range(10):
            s[10 * t + r, 16 * t + r] = 1
        for i in range(2):
            s[80 + 2 * t + i, 16 * t + 10 + i] = 1
    return s


def part_rows():
    s = np.zeros((640, 640), np.float32)
    for t in range(8):
        for q in range(8):
            for i in range(5):
                s[80 * t + 5 * q + i, 80 * q + 10 * t + i] = 1
                s[80 * t + 40 + 5 * q + i, 80 * q + 10 * t + 5 + i] = 1
    return s


def reference_rows():
    s = np.zeros((256, 256), np.float32)
    for t in range(8):
        for q in range(Z):
            for i in range(2):
                s[32 * t + 2 * q + i, 16 * q + 2 * t + i] = 1
    return s


def pack_rows():
    s = np.zeros((384, 320), np.float32)
    for p in range(8):
        for t in range(4):
            for i in range(10):
                s[p * 48 + 10 * t + i, 80 * t + 40 * (i // 5) + 5 * p + i % 5] = 1
    return s


def row_table():
    t = np.zeros((160, 128), np.int32)
    for r in range(160):
        t[r, 0] = OFFSETS[8 * (r // 80) + r % 40 // 5]
        t[r, 1] = 5 * (r % 80 // 40) + r % 5
    return t


def kernel(
    ex_ref, rf_ref, ct_ref, wg_hbm, wu_hbm, wd_hbm, pair_ref, points_ref,
    sel0_ref, perm_hbm, rperm_hbm, pack_hbm, table_ref,
    out_ref,
    wg, wu, wd, perm, rperm, pack, wcat, wd2, xbuf, rbuf, xs, xr, sendb, recvb, sendr, recvr, onehot, base, acce, accu,
    bdiag, sendc, full, d1send, d1recv, keep, d2send, d2recv, d3send, d3recv, fin, finr,
    wsem, zs, zr, ws, wr, ys, yr, hs, hr, ms, mr, gs, gr, bs, br, cs, cr, d1s, d1r, d2s, d2r, d3s, d3r, fs, fr,
):
    h, z, c = lax.axis_index("h"), lax.axis_index("z"), lax.axis_index("c")
    x, l = lax.axis_index("x"), lax.axis_index("l")
    mine = 2 * x + l
    m, mh = 2 * h + c, 2 * (1 - h) + c
    pending = []

    def send(src, dst, ssem, rsem, dev):
        cp = pltpu.make_async_remote_copy(
            src_ref=src, dst_ref=dst, send_sem=ssem, recv_sem=rsem, device_id=dev, device_id_type=MESH
        )
        cp.start()
        pending.append(cp)
        return cp

    def along(offset):
        return {"z": lax.rem(z + offset + Z, Z)}

    facing, mate = {"h": 1 - h}, {"c": 1 - c}
    peers = [{"x": lax.rem(x + i // 2, 4), "l": lax.rem(l + i % 2, 2)} for i in range(8)]
    barrier = pltpu.get_barrier_semaphore()
    for dev in [along(e) for e in (8, 4, -4, 2, -2, 1, -1)] + [facing] + peers[1:] + [mate]:
        pl.semaphore_signal(barrier, inc=1, device_id=dev, device_id_type=MESH)

    loads = [
        pltpu.make_async_copy(a, b, wsem.at[i])
        for i, (a, b) in enumerate(((wg_hbm, wg), (wu_hbm, wu), (wd_hbm, wd), (perm_hbm, perm), (rperm_hbm, rperm), (pack_hbm, pack)))
    ]
    for cp in loads:
        cp.start()

    t = jnp.concatenate(
        [ex_ref[...].astype(F32), ct_ref[...].astype(F32), rf_ref[...].astype(F32), jnp.zeros((4, 1024), F32)], axis=0
    ).astype(BF)
    t = jnp.concatenate([t[:, 128 * i : 128 * i + 128] for i in range(8)], axis=0)
    t = dot(sel0_ref[...], t).astype(BF)
    xbuf[0, m, 0] = t[:80]
    rbuf[m, 0] = t[80:]
    pl.semaphore_wait(barrier, 16)

    def block(p, who):
        return xbuf.at[p // 8, who, p % 8]

    zc, wc, yc = {}, {}, {}

    def zsend(offset, e):
        p = slot_of(offset - e)
        zc[p] = send(block(slot_of(offset), m), block(p, m), zs.at[p], zr.at[p], along(e))

    def ysend(offset, e):
        p = slot_of(offset - e)
        yc[p] = send(block(slot_of(offset), mh), block(p, mh), ys.at[p], yr.at[p], along(e))

    def wsend(offset, e):
        p = slot_of(offset - e)
        wc[p] = send(rbuf.at[m, slot_of(offset)], rbuf.at[m, p], ws.at[p], wr.at[p], along(e))

    for e in (8, 4, -4, 2, -2, 1, -1):
        wsend(0, e)
    for e in (8, 4, -4):
        zsend(0, e)

    for cp in loads:
        cp.wait()

    def prep(a):
        w0 = (0, 0, 128, 256)[a]
        kk = min(256, 448 - w0)
        k = lax.broadcasted_iota(jnp.int32, (256, kk), 1) + w0
        n = lax.broadcasted_iota(jnp.int32, (256, kk), 0)
        r = n & 127
        first = 56 * (2 * a + (n >> 7))
        gate = (r < 56) & (k == first + r)
        up = (r >= 64) & (r < 120) & (k == first + r - 64)
        sg = jnp.where(gate, 1.0, 0.0).astype(BF)
        su = jnp.where(up, 1.0, 0.0).astype(BF)
        sd = jnp.where(gate | up, 1.0, 0.0).astype(BF)
        for b in range(4):
            cols = pl.ds(256 * b, 256)
            rows = pl.ds(w0, kk)
            wcat[pl.ds(256 * a, 256), cols] = (dot(sg, wg[rows, cols]) + dot(su, wu[rows, cols])).astype(BF)
            wd2[pl.ds(256 * a, 256), cols] = dot(sd, wd[rows, cols]).astype(BF)

    hc, mc, gc = {}, {}, {}

    groups = ((0, 1), (1, 5), (5, 8), (8, 12), (12, 16), (0, 8), (8, 16))

    def group(k, who):
        first, last = groups[k]
        if k > 4:
            return rbuf.at[who, pl.ds(first, last - first)]
        return xbuf.at[first // 8, who, pl.ds(first % 8, last - first)]

    def spread(k):
        for p in range(*groups[k]):
            if p not in (0, 5, 6, 7):
                (wc if k > 4 else zc)[p].wait_recv()
        at = group(k, m)
        if k not in (3, 4):
            hc[k] = send(at, at, hs.at[k], hr.at[k], facing)
        mc[k] = send(at, at, ms.at[k], mr.at[k], mate)

    def onward(k):
        if k in (3, 4):
            for p in range(*groups[k]):
                yc[p].wait_recv()
        else:
            hc[k].wait_recv()
        at = group(k, mh)
        gc[k] = send(at, at, gs.at[k], gr.at[k], mate)

    def to_owners(src, dst, at):
        for i in (7, 5, 3, 4, 1, 6, 2):
            n = 8 * at + i
            to = src.at[lax.rem(x + i // 2, 4), lax.rem(l + i % 2, 2)]
            bc[at, i] = send(to, dst.at[i], bs.at[n], br.at[n], peers[i])

    def reference_work():
        for g in (5, 6):
            mc[g].wait_recv()
            gc[g].wait_recv()
        for i in range(4):
            o = dot(rperm[...], rbuf[i].reshape(256, 128)).astype(BF)
            for t in range(8):
                xr[32 * i : 32 * i + 32, 128 * t : 128 * t + 128] = o[32 * t : 32 * t + 32]

        @pl.loop(0, 4)
        def _(n):
            cols = pl.ds(pl.multiple_of(256 * n, 256), 256)
            p = dot_nt(xr[...], wcat[cols, :]).astype(BF)
            for e in range(2):
                sendr[n, e] = p[:, 128 * e : 128 * e + 128]

        to_owners(sendr, recvr, 2)

    def work(k):
        for g in ((0, 1, 2), (3, 4))[k]:
            mc[g].wait_recv()
            gc[g].wait_recv()
        for i in range(2):
            o = [dot(perm[...], xbuf[k, 2 * i + j].reshape(640, 128)) for j in range(2)]
            for t in range(8):
                for b in range(2):
                    rows = slice(80 * t + 40 * b, 80 * t + 40 * b + 40)
                    at = slice(160 * b + 80 * i, 160 * b + 80 * i + 80)
                    xs[at, 128 * t : 128 * t + 128] = jnp.concatenate([o[0][rows], o[1][rows]], axis=0).astype(BF)
        left = lax.broadcasted_iota(jnp.int32, (80, 256), 1) & 127

        @pl.loop(0, 4)
        def _(n):
            cols = pl.ds(pl.multiple_of(256 * n, 256), 256)
            p = dot_nt(xs[0:160], wcat[cols, :]).astype(BF)
            d = dot_nt(xs[160:320], wd2[cols, :])
            d = jnp.where(left < 64, d[:80], d[80:]).astype(BF)
            for e in range(2):
                sendb[k, n, e, 0:160] = p[:, 128 * e : 128 * e + 128]
                sendb[k, n, e, 160:240] = d[:, 128 * e : 128 * e + 128]

        to_owners(sendb.at[k], recvb.at[k], k)

    bc = {}

    def owner_sum(k):
        total = sendb[k, x, l].astype(F32)
        for i in range(1, 8):
            bc[k, i].wait_recv()
            total = total + recvb[k, i].astype(F32)
        e0, e1 = total[0:80], total[80:160]
        half = lax.broadcasted_iota(jnp.int32, (80, 128), 1) < 64
        acce[0, 80 * k : 80 * k + 80] = jnp.where(half, e0, pltpu.roll(e1, 64, 1))
        acce[1, 80 * k : 80 * k + 80] = jnp.where(half, pltpu.roll(e0, 64, 1), e1)
        accu[80 * k : 80 * k + 80] = total[160:240]

    def choose():
        off, place = table_ref[:, 0:1], table_ref[:, 1:2]
        want = ((z + off + Z) & (Z - 1)) * 10 + place
        turn = jnp.where(lax.broadcasted_iota(jnp.int32, (160, 160), 1) == want, 1.0, 0.0).astype(BF)
        for hh in range(2):
            picks = pair_ref[...].astype(F32)[:, 160 * hh : 160 * hh + 160].astype(BF)
            r = dot_nt(turn, picks).astype(jnp.int32)
            delta = (((r >> 2) & 15) - z + Z) & (Z - 1)
            slot = jnp.zeros_like(delta)
            for p in range(1, Z):
                slot = jnp.where(delta == OFFSETS[p] % Z, p, slot)
            pos = (r >> 6) * 64 + ((r >> 1) & 1) * 32 + slot * 2 + (r & 1)
            lane = lax.broadcasted_iota(jnp.int32, (160, 128), 1)
            for p in range(4):
                onehot[p, :, 128 * hh : 128 * hh + 128] = jnp.where(lane == pos[:, p : p + 1], 1.0, 0.0).astype(BF)

    spread(0)
    for i in range(4):
        prep(i)
    for e in (2, -2, 1, -1):
        zsend(0, e)
    def near(far, to):
        for offset, e in {
            7: ((8, 1), (8, -1)), 5: ((4, -2), (4, 1), (4, -1)), 6: ((-4, 2), (-4, 1), (-4, -1))
        }[far]:
            to(offset, e)

    for got, to in ((wc, wsend), (zc, zsend)):
        for p in (7, 5, 6):
            got[p].wait_recv()
            near(p, to)
    spread(2)
    spread(5)
    choose()
    onward(2)
    for p in (7, 5, 6):
        near(p, ysend)
    spread(1)
    spread(6)
    onward(0)
    onward(5)
    onward(6)
    reference_work()
    onward(1)
    spread(3)
    spread(4)
    work(0)
    onward(3)
    onward(4)
    work(1)

    def bases():
        refs = sendr[x, l].astype(F32)
        for i in range(1, 8):
            bc[2, i].wait_recv()
            refs = refs + recvr[i].astype(F32)
        turned = pltpu.roll(refs, 64, 1)
        left = lax.broadcasted_iota(jnp.int32, (128, 128), 1) < 64
        diag = (
            jnp.where(left, refs, 0.0), jnp.where(left, 0.0, turned),
            jnp.where(left, turned, 0.0), jnp.where(left, 0.0, refs),
        )
        for n, block in enumerate(diag):
            high = block.astype(BF)
            low = (block - high.astype(F32)).astype(BF)
            at = (slice(128 * (n % 2), 128 * (n % 2) + 128), slice(128 * (n // 2), 128 * (n // 2) + 128))
            bdiag[(0, *at)] = high
            bdiag[(1, *at)] = low
        for p in range(4):
            base[p] = dot(onehot[p], bdiag[0]) + dot(onehot[p], bdiag[1])

    bases()
    owner_sum(0)

    alphas = [points_ref[i].astype(F32) * 0.125 for i in range(8)]

    lanes = pl.ds(pl.multiple_of(128 * mine, 128), 128)
    cc = {}

    def coefs(part):
        @pl.loop(0, 5)
        def _(n):
            rows = pl.ds(pl.multiple_of(80 * part + 16 * n, 16), 16)
            eg, eu, up = acce[0, rows], acce[1, rows], accu[rows]
            cg = jnp.zeros((16, 128), F32)
            cu = jnp.zeros((16, 128), F32)
            for p in range(4):
                bg, bu = base[p, rows, 0:128], base[p, rows, 128:256]
                dg, du = eg - bg, eu - bu
                for a in alphas:
                    g = bg + a * dg
                    u = bu + a * du
                    s = 0.5 * jnp.tanh(0.5 * g) + 0.5
                    gs = g * s
                    cu = cu + gs
                    cg = cg + u * (s + gs * (1.0 - s))
            cg = up * (cg * (1.0 / 32.0))
            cu = up * (cu * (1.0 / 32.0))
            half = lax.broadcasted_iota(jnp.int32, (16, 128), 1) < 64
            first = pl.ds(pl.multiple_of(16 * n, 16), 16)
            second = pl.ds(pl.multiple_of(80 + 16 * n, 16), 16)
            sendc[part, first, :] = jnp.where(half, cg, pltpu.roll(cu, 64, 1)).astype(BF)
            sendc[part, second, :] = jnp.where(half, pltpu.roll(cg, 64, 1), cu).astype(BF)

        for i in range(1, 8):
            n = 8 * part + i
            cc[part, i] = send(sendc.at[part], full.at[part, :, lanes], cs.at[n], cr.at[n], peers[i])
        full[part, :, lanes] = sendc[part]

    def product(part, hh, col, into, at):
        rows = pl.ds(pl.multiple_of(80 * hh, 16), 80)

        @pl.loop(0, 2)
        def _(n):
            w = pl.ds(pl.multiple_of(512 * col + 256 * n, 256), 256)
            into[at, :, pl.ds(pl.multiple_of(256 * n, 256), 256)] = dot(full[part, rows, :], wcat[:, w])

    d1, d2, d3 = {}, {}, {}

    def products(part):
        for i in range(1, 8):
            cc[part, i].wait_recv()
        for i, hh in enumerate((1 - h, h)):
            at = 2 * part + i
            product(part, hh, 1 - c, d1send, at)
            d1[at] = send(d1send.at[at], d1recv.at[at], d1s.at[at], d1r.at[at], mate)
            product(part, hh, c, keep, at)

    def face(part):
        d1[2 * part].wait_recv()
        d2send[part] = (keep[2 * part] + d1recv[2 * part]).astype(BF)
        d2[part] = send(d2send.at[part], d2recv.at[part], d2s.at[part], d2r.at[part], facing)

    def scatter(part):
        d1[2 * part + 1].wait_recv()
        v = keep[2 * part + 1] + d1recv[2 * part + 1]
        d2[part].wait_recv()
        v = (v + d2recv[part].astype(F32)).astype(BF)
        v = jnp.concatenate([v[:, 128 * t : 128 * t + 128] for t in range(4)], axis=0)
        d3send[8 * part : 8 * part + 8] = dot(pack[...], v).astype(BF).reshape(8, 48, 128)
        for p in range(8 * part, 8 * part + 8):
            if p:
                d3[p] = send(d3send.at[p], d3recv.at[p], d3s.at[p], d3r.at[p], along(OFFSETS[p]))

    coefs(0)
    owner_sum(1)
    coefs(1)
    for part in range(2):
        products(part)
        face(part)
    scatter(0)
    scatter(1)
    total = d3send[0].astype(F32)
    for p in range(1, Z):
        d3[p].wait_recv()
        total = total + d3recv[p].astype(F32)
    fin[...] = total
    last = send(fin, finr, fs, fr, mate)
    last.wait_recv()
    other = finr[...]
    first = c == 0
    parts = []
    for block in (jnp.where(first, total, other), jnp.where(first, other, total)):
        for t in range(4):
            parts.append(jnp.where(first, block[10 * t : 10 * t + 5], block[10 * t + 5 : 10 * t + 10]))
    out_ref[...] = jnp.concatenate(parts, axis=1).astype(BF)
    for cp in pending:
        cp.wait_send()


def on_device(examples, references, gate_weight, up_weight, down_weight, cotangent, pair_ref, points):
    vm = pl.BlockSpec(memory_space=pltpu.VMEM)
    hbm = pl.BlockSpec(memory_space=pltpu.HBM)
    sm = pl.BlockSpec(memory_space=pltpu.SMEM)
    dma = pltpu.SemaphoreType.DMA
    V = pltpu.VMEM
    return pl.pallas_call(
        kernel,
        out_shape=jax.ShapeDtypeStruct((5, 1024), BF),
        in_specs=[vm, vm, vm, hbm, hbm, hbm, vm, sm, vm, hbm, hbm, hbm, vm],
        out_specs=vm,
        scratch_shapes=[
            V((448, 1024), BF), V((448, 1024), BF), V((448, 1024), BF),
            V((640, 640), BF), V((256, 256), BF), V((384, 320), BF),
            V((1024, 1024), BF), V((1024, 1024), BF),
            V((2, 4, 8, 80, 128), BF), V((4, Z, 16, 128), BF), V((320, 1024), BF), V((128, 1024), BF),
            V((2, 4, 2, 240, 128), BF), V((2, 8, 240, 128), BF),
            V((4, 2, 128, 128), BF), V((8, 128, 128), BF),
            V((4, 160, 256), BF), V((4, 160, 256), F32),
            V((2, 160, 128), F32), V((160, 128), F32),
            V((2, 256, 256), BF), V((2, 160, 128), BF), V((2, 160, 1024), BF),
            V((4, 80, 512), F32), V((4, 80, 512), F32), V((4, 80, 512), F32),
            V((2, 80, 512), BF), V((2, 80, 512), BF),
            V((Z, 48, 128), BF), V((Z, 48, 128), BF), V((48, 128), F32), V((48, 128), F32),
            dma((6,)), dma((Z,)), dma((Z,)), dma((Z,)), dma((Z,)), dma((Z,)), dma((Z,)), dma((7,)), dma((7,)), dma((7,)), dma((7,)),
            dma((7,)), dma((7,)), dma((24,)), dma((24,)), dma((16,)), dma((16,)), dma((4,)), dma((4,)),
            dma((2,)), dma((2,)), dma((Z,)), dma((Z,)), dma, dma,
        ],
        compiler_params=pltpu.CompilerParams(
            collective_id=0, has_side_effects=True, vmem_limit_bytes=60 * 1024 * 1024
        ),
        cost_estimate=pl.CostEstimate(flops=2 * 10**9, bytes_accessed=4 * 10**6, transcendentals=10**6),
    )(
        examples, references, cotangent, gate_weight.T, up_weight.T, down_weight, pair_ref.T, points,
        jnp.asarray(compact_rows(), BF), jnp.asarray(part_rows(), BF), jnp.asarray(reference_rows(), BF),
        jnp.asarray(pack_rows(), BF), jnp.asarray(row_table()),
    )


def solution(mesh):
    split = Mesh(mesh.devices.reshape(2, Z, 2, 4, 2), ("h", "z", "c", "x", "l"))
    wide, narrow = ("h", "z", "c"), ("x", "l")
    return jax.shard_map(
        on_device,
        mesh=split,
        in_specs=(
            P(wide, narrow), P(wide, narrow), P(narrow, wide), P(narrow, wide),
            P(wide, narrow), P(wide, narrow), P(), P(),
        ),
        out_specs=P(wide, narrow),
        check_vma=False,
    )
```

```python
import functools

import jax
import jax.numpy as jnp
import numpy as np
from jax import lax
from jax.experimental import pallas as pl
from jax.experimental.pallas import tpu as pltpu
from jax.sharding import Mesh
from jax.sharding import PartitionSpec as P

MESH = pl.DeviceIdType.MESH
BF = jnp.bfloat16
F32 = jnp.float32
Z = 16
NT = (((1,), (1,)), ((), ()))


def dot(a, b):
    return jnp.dot(a, b, preferred_element_type=F32)


def dot_nt(a, b):
    return lax.dot_general(a, b, NT, preferred_element_type=F32)


OFFSETS = (0, 1, -1, 2, -2, 4, -4, 8, 3, -3, 5, -5, 6, -6, 7, -7)


def slot_of(offset):
    return next(p for p in range(Z) if (OFFSETS[p] - offset) % Z == 0)


def compact_rows():
    s = np.zeros((96, 128), np.float32)
    for t in range(8):
        for r in range(10):
            s[10 * t + r, 16 * t + r] = 1
        for i in range(2):
            s[80 + 2 * t + i, 16 * t + 10 + i] = 1
    return s


def part_rows():
    s = np.zeros((640, 640), np.float32)
    for t in range(8):
        for q in range(8):
            for i in range(5):
                s[80 * t + 5 * q + i, 80 * q + 10 * t + i] = 1
                s[80 * t + 40 + 5 * q + i, 80 * q + 10 * t + 5 + i] = 1
    return s


def reference_rows():
    s = np.zeros((256, 256), np.float32)
    for t in range(8):
        for q in range(Z):
            for i in range(2):
                s[32 * t + 2 * q + i, 16 * q + 2 * t + i] = 1
    return s


def pack_rows():
    s = np.zeros((384, 320), np.float32)
    for p in range(8):
        for t in range(4):
            for i in range(10):
                s[p * 48 + 10 * t + i, 80 * t + 40 * (i // 5) + 5 * p + i % 5] = 1
    return s


def row_table():
    t = np.zeros((160, 128), np.int32)
    for r in range(160):
        t[r, 0] = OFFSETS[8 * (r // 80) + r % 40 // 5]
        t[r, 1] = 5 * (r % 80 // 40) + r % 5
    return t


def kernel(
    ex_ref, rf_ref, ct_ref, wg_hbm, wu_hbm, wd_hbm, pair_ref, points_ref,
    sel0_ref, perm_hbm, rperm_hbm, pack_hbm, table_ref,
    out_ref,
    wg, wu, wd, perm, rperm, pack, wcat, wd2, xbuf, rbuf, xs, xr, sendb, recvb, sendr, recvr, onehot, base, acce, accu,
    bdiag, sendc, full, d1send, d1recv, keep, d2send, d2recv, d3send, d3recv, fin, finr,
    wsem, zs, zr, ws, wr, ys, yr, hs, hr, ms, mr, gs, gr, bs, br, cs, cr, d1s, d1r, d2s, d2r, d3s, d3r, fs, fr,
):
    h, z, c = lax.axis_index("h"), lax.axis_index("z"), lax.axis_index("c")
    x, l = lax.axis_index("x"), lax.axis_index("l")
    mine = 2 * x + l
    m, mh = 2 * h + c, 2 * (1 - h) + c
    pending = []

    def send(src, dst, ssem, rsem, dev):
        cp = pltpu.make_async_remote_copy(
            src_ref=src, dst_ref=dst, send_sem=ssem, recv_sem=rsem, device_id=dev, device_id_type=MESH
        )
        cp.start()
        pending.append(cp)
        return cp

    def along(offset):
        return {"z": lax.rem(z + offset + Z, Z)}

    facing, mate = {"h": 1 - h}, {"c": 1 - c}
    peers = [{"x": lax.rem(x + i // 2, 4), "l": lax.rem(l + i % 2, 2)} for i in range(8)]
    barrier = pltpu.get_barrier_semaphore()
    for dev in [along(e) for e in (8, 4, -4, 2, -2, 1, -1)] + [facing] + peers[1:] + [mate]:
        pl.semaphore_signal(barrier, inc=1, device_id=dev, device_id_type=MESH)

    loads = [
        pltpu.make_async_copy(a, b, wsem.at[i])
        for i, (a, b) in enumerate(((wg_hbm, wg), (wu_hbm, wu), (wd_hbm, wd), (perm_hbm, perm), (rperm_hbm, rperm), (pack_hbm, pack)))
    ]
    for cp in loads:
        cp.start()

    t = jnp.concatenate(
        [ex_ref[...].astype(F32), ct_ref[...].astype(F32), rf_ref[...].astype(F32), jnp.zeros((4, 1024), F32)], axis=0
    ).astype(BF)
    t = jnp.concatenate([t[:, 128 * i : 128 * i + 128] for i in range(8)], axis=0)
    t = dot(sel0_ref[...], t).astype(BF)
    xbuf[0, m, 0] = t[:80]
    rbuf[m, 0] = t[80:]
    pl.semaphore_wait(barrier, 16)

    def block(p, who):
        return xbuf.at[p // 8, who, p % 8]

    zc, wc, yc = {}, {}, {}

    def zsend(offset, e):
        p = slot_of(offset - e)
        zc[p] = send(block(slot_of(offset), m), block(p, m), zs.at[p], zr.at[p], along(e))

    def ysend(offset, e):
        p = slot_of(offset - e)
        yc[p] = send(block(slot_of(offset), mh), block(p, mh), ys.at[p], yr.at[p], along(e))

    def wsend(offset, e):
        p = slot_of(offset - e)
        wc[p] = send(rbuf.at[m, slot_of(offset)], rbuf.at[m, p], ws.at[p], wr.at[p], along(e))

    for e in (8, 4, -4, 2, -2, 1, -1):
        wsend(0, e)
    for e in (8, 4, -4):
        zsend(0, e)

    for cp in loads:
        cp.wait()

    def prep(a):
        w0 = (0, 0, 128, 256)[a]
        kk = min(256, 448 - w0)
        k = lax.broadcasted_iota(jnp.int32, (256, kk), 1) + w0
        n = lax.broadcasted_iota(jnp.int32, (256, kk), 0)
        r = n & 127
        first = 56 * (2 * a + (n >> 7))
        gate = (r < 56) & (k == first + r)
        up = (r >= 64) & (r < 120) & (k == first + r - 64)
        sg = jnp.where(gate, 1.0, 0.0).astype(BF)
        su = jnp.where(up, 1.0, 0.0).astype(BF)
        sd = jnp.where(gate | up, 1.0, 0.0).astype(BF)
        for b in range(4):
            cols = pl.ds(256 * b, 256)
            rows = pl.ds(w0, kk)
            wcat[pl.ds(256 * a, 256), cols] = (dot(sg, wg[rows, cols]) + dot(su, wu[rows, cols])).astype(BF)
            wd2[pl.ds(256 * a, 256), cols] = dot(sd, wd[rows, cols]).astype(BF)

    hc, mc, gc = {}, {}, {}

    groups = ((0, 1), (1, 5), (5, 8), (8, 12), (12, 16), (0, 8), (8, 16))

    def group(k, who):
        first, last = groups[k]
        if k > 4:
            return rbuf.at[who, pl.ds(first, last - first)]
        return xbuf.at[first // 8, who, pl.ds(first % 8, last - first)]

    def spread(k):
        for p in range(*groups[k]):
            if p not in (0, 5, 6, 7):
                (wc if k > 4 else zc)[p].wait_recv()
        at = group(k, m)
        if k not in (3, 4):
            hc[k] = send(at, at, hs.at[k], hr.at[k], facing)
        mc[k] = send(at, at, ms.at[k], mr.at[k], mate)

    def onward(k):
        if k in (3, 4):
            for p in range(*groups[k]):
                yc[p].wait_recv()
        else:
            hc[k].wait_recv()
        at = group(k, mh)
        gc[k] = send(at, at, gs.at[k], gr.at[k], mate)

    def to_owners(src, dst, at):
        for i in (7, 5, 3, 4, 1, 6, 2):
            n = 8 * at + i
            to = src.at[lax.rem(x + i // 2, 4), lax.rem(l + i % 2, 2)]
            bc[at, i] = send(to, dst.at[i], bs.at[n], br.at[n], peers[i])

    def reference_work():
        for g in (5, 6):
            mc[g].wait_recv()
            gc[g].wait_recv()
        for i in range(4):
            o = dot(rperm[...], rbuf[i].reshape(256, 128)).astype(BF)
            for t in range(8):
                xr[32 * i : 32 * i + 32, 128 * t : 128 * t + 128] = o[32 * t : 32 * t + 32]

        @pl.loop(0, 4)
        def _(n):
            cols = pl.ds(pl.multiple_of(256 * n, 256), 256)
            p = dot_nt(xr[...], wcat[cols, :]).astype(BF)
            for e in range(2):
                sendr[n, e] = p[:, 128 * e : 128 * e + 128]

        to_owners(sendr, recvr, 2)

    def work(k):
        for g in ((0, 1, 2), (3, 4))[k]:
            mc[g].wait_recv()
            gc[g].wait_recv()
        for i in range(2):
            o = [dot(perm[...], xbuf[k, 2 * i + j].reshape(640, 128)) for j in range(2)]
            for t in range(8):
                for b in range(2):
                    rows = slice(80 * t + 40 * b, 80 * t + 40 * b + 40)
                    at = slice(160 * b + 80 * i, 160 * b + 80 * i + 80)
                    xs[at, 128 * t : 128 * t + 128] = jnp.concatenate([o[0][rows], o[1][rows]], axis=0).astype(BF)
        left = lax.broadcasted_iota(jnp.int32, (80, 256), 1) & 127

        @pl.loop(0, 4)
        def _(n):
            cols = pl.ds(pl.multiple_of(256 * n, 256), 256)
            p = dot_nt(xs[0:160], wcat[cols, :]).astype(BF)
            d = dot_nt(xs[160:320], wd2[cols, :])
            d = jnp.where(left < 64, d[:80], d[80:]).astype(BF)
            for e in range(2):
                sendb[k, n, e, 0:160] = p[:, 128 * e : 128 * e + 128]
                sendb[k, n, e, 160:240] = d[:, 128 * e : 128 * e + 128]

        to_owners(sendb.at[k], recvb.at[k], k)

    bc = {}

    def owner_sum(k):
        total = sendb[k, x, l].astype(F32)
        for i in range(1, 8):
            bc[k, i].wait_recv()
            total = total + recvb[k, i].astype(F32)
        e0, e1 = total[0:80], total[80:160]
        half = lax.broadcasted_iota(jnp.int32, (80, 128), 1) < 64
        acce[0, 80 * k : 80 * k + 80] = jnp.where(half, e0, pltpu.roll(e1, 64, 1))
        acce[1, 80 * k : 80 * k + 80] = jnp.where(half, pltpu.roll(e0, 64, 1), e1)
        accu[80 * k : 80 * k + 80] = total[160:240]

    def choose():
        off, place = table_ref[:, 0:1], table_ref[:, 1:2]
        want = ((z + off + Z) & (Z - 1)) * 10 + place
        turn = jnp.where(lax.broadcasted_iota(jnp.int32, (160, 160), 1) == want, 1.0, 0.0).astype(BF)
        for hh in range(2):
            picks = pair_ref[...].astype(F32)[:, 160 * hh : 160 * hh + 160].astype(BF)
            r = dot_nt(turn, picks).astype(jnp.int32)
            delta = (((r >> 2) & 15) - z + Z) & (Z - 1)
            slot = jnp.zeros_like(delta)
            for p in range(1, Z):
                slot = jnp.where(delta == OFFSETS[p] % Z, p, slot)
            pos = (r >> 6) * 64 + ((r >> 1) & 1) * 32 + slot * 2 + (r & 1)
            lane = lax.broadcasted_iota(jnp.int32, (160, 128), 1)
            for p in range(4):
                onehot[p, :, 128 * hh : 128 * hh + 128] = jnp.where(lane == pos[:, p : p + 1], 1.0, 0.0).astype(BF)

    spread(0)
    for i in range(4):
        prep(i)
    for e in (2, -2, 1, -1):
        zsend(0, e)
    def near(far, to):
        for offset, e in {
            7: ((8, 1), (8, -1)), 5: ((4, -2), (4, 1), (4, -1)), 6: ((-4, 2), (-4, 1), (-4, -1))
        }[far]:
            to(offset, e)

    for got, to in ((wc, wsend), (zc, zsend)):
        for p in (7, 5, 6):
            got[p].wait_recv()
            near(p, to)
    spread(2)
    spread(5)
    choose()
    onward(2)
    for p in (7, 5, 6):
        near(p, ysend)
    spread(1)
    spread(6)
    onward(0)
    onward(5)
    onward(6)
    reference_work()
    onward(1)
    spread(3)
    spread(4)
    work(0)
    onward(3)
    onward(4)
    work(1)

    def bases():
        refs = sendr[x, l].astype(F32)
        for i in range(1, 8):
            bc[2, i].wait_recv()
            refs = refs + recvr[i].astype(F32)
        turned = pltpu.roll(refs, 64, 1)
        left = lax.broadcasted_iota(jnp.int32, (128, 128), 1) < 64
        diag = (
            jnp.where(left, refs, 0.0), jnp.where(left, 0.0, turned),
            jnp.where(left, turned, 0.0), jnp.where(left, 0.0, refs),
        )
        for n, block in enumerate(diag):
            high = block.astype(BF)
            low = (block - high.astype(F32)).astype(BF)
            at = (slice(128 * (n % 2), 128 * (n % 2) + 128), slice(128 * (n // 2), 128 * (n // 2) + 128))
            bdiag[(0, *at)] = high
            bdiag[(1, *at)] = low
        for p in range(4):
            base[p] = dot(onehot[p], bdiag[0]) + dot(onehot[p], bdiag[1])

    bases()
    owner_sum(0)

    alphas = [points_ref[i].astype(F32) * 0.125 for i in range(8)]

    lanes = pl.ds(pl.multiple_of(128 * mine, 128), 128)
    cc = {}

    def coefs(part):
        @pl.loop(0, 5)
        def _(n):
            rows = pl.ds(pl.multiple_of(80 * part + 16 * n, 16), 16)
            eg, eu, up = acce[0, rows], acce[1, rows], accu[rows]
            cg = jnp.zeros((16, 128), F32)
            cu = jnp.zeros((16, 128), F32)
            for p in range(4):
                bg, bu = base[p, rows, 0:128], base[p, rows, 128:256]
                dg, du = eg - bg, eu - bu
                for a in alphas:
                    g = bg + a * dg
                    u = bu + a * du
                    s = 0.5 * jnp.tanh(0.5 * g) + 0.5
                    gs = g * s
                    cu = cu + gs
                    cg = cg + u * (s + gs * (1.0 - s))
            cg = up * (cg * (1.0 / 32.0))
            cu = up * (cu * (1.0 / 32.0))
            half = lax.broadcasted_iota(jnp.int32, (16, 128), 1) < 64
            first = pl.ds(pl.multiple_of(16 * n, 16), 16)
            second = pl.ds(pl.multiple_of(80 + 16 * n, 16), 16)
            sendc[part, first, :] = jnp.where(half, cg, pltpu.roll(cu, 64, 1)).astype(BF)
            sendc[part, second, :] = jnp.where(half, pltpu.roll(cg, 64, 1), cu).astype(BF)

        for b, hh in enumerate((1 - h, h)):
            rows = pl.ds(pl.multiple_of(80 * hh, 16), 80)
            for i in range(1, 8):
                n = 16 * part + 8 * b + i
                cc[part, b, i] = send(
                    sendc.at[part, rows], full.at[part, rows, lanes], cs.at[n], cr.at[n], peers[i]
                )
        full[part, :, lanes] = sendc[part]

    def product(part, hh, col, into, at):
        rows = pl.ds(pl.multiple_of(80 * hh, 16), 80)

        @pl.loop(0, 2)
        def _(n):
            w = pl.ds(pl.multiple_of(512 * col + 256 * n, 256), 256)
            into[at, :, pl.ds(pl.multiple_of(256 * n, 256), 256)] = dot(full[part, rows, :], wcat[:, w])

    d1, d2, d3 = {}, {}, {}

    def products(part):
        for i in range(1, 8):
            cc[part, 0, i].wait_recv()
        at = 2 * part

        def lend(i, hh):
            product(part, hh, 1 - c, d1send, at + i)
            d1[at + i] = send(d1send.at[at + i], d1recv.at[at + i], d1s.at[at + i], d1r.at[at + i], mate)

        lend(0, 1 - h)
        product(part, 1 - h, c, keep, at)
        d1[at].wait_recv()
        d2send[part] = (keep[at] + d1recv[at]).astype(BF)
        d2[part] = send(d2send.at[part], d2recv.at[part], d2s.at[part], d2r.at[part], facing)
        for i in range(1, 8):
            cc[part, 1, i].wait_recv()
        lend(1, h)
        product(part, h, c, keep, at + 1)

    def scatter(part):
        d1[2 * part + 1].wait_recv()
        v = keep[2 * part + 1] + d1recv[2 * part + 1]
        d2[part].wait_recv()
        v = (v + d2recv[part].astype(F32)).astype(BF)
        v = jnp.concatenate([v[:, 128 * t : 128 * t + 128] for t in range(4)], axis=0)
        d3send[8 * part : 8 * part + 8] = dot(pack[...], v).astype(BF).reshape(8, 48, 128)
        for p in range(8 * part, 8 * part + 8):
            if p:
                d3[p] = send(d3send.at[p], d3recv.at[p], d3s.at[p], d3r.at[p], along(OFFSETS[p]))

    coefs(0)
    owner_sum(1)
    coefs(1)
    products(0)
    products(1)
    scatter(0)
    scatter(1)
    total = d3send[0].astype(F32)
    for p in range(1, Z):
        d3[p].wait_recv()
        total = total + d3recv[p].astype(F32)
    fin[...] = total
    last = send(fin, finr, fs, fr, mate)
    last.wait_recv()
    other = finr[...]
    first = c == 0
    parts = []
    for block in (jnp.where(first, total, other), jnp.where(first, other, total)):
        for t in range(4):
            parts.append(jnp.where(first, block[10 * t : 10 * t + 5], block[10 * t + 5 : 10 * t + 10]))
    out_ref[...] = jnp.concatenate(parts, axis=1).astype(BF)
    for cp in pending:
        cp.wait_send()


def on_device(examples, references, gate_weight, up_weight, down_weight, cotangent, pair_ref, points):
    vm = pl.BlockSpec(memory_space=pltpu.VMEM)
    hbm = pl.BlockSpec(memory_space=pltpu.HBM)
    sm = pl.BlockSpec(memory_space=pltpu.SMEM)
    dma = pltpu.SemaphoreType.DMA
    V = pltpu.VMEM
    return pl.pallas_call(
        kernel,
        out_shape=jax.ShapeDtypeStruct((5, 1024), BF),
        in_specs=[vm, vm, vm, hbm, hbm, hbm, vm, sm, vm, hbm, hbm, hbm, vm],
        out_specs=vm,
        scratch_shapes=[
            V((448, 1024), BF), V((448, 1024), BF), V((448, 1024), BF),
            V((640, 640), BF), V((256, 256), BF), V((384, 320), BF),
            V((1024, 1024), BF), V((1024, 1024), BF),
            V((2, 4, 8, 80, 128), BF), V((4, Z, 16, 128), BF), V((320, 1024), BF), V((128, 1024), BF),
            V((2, 4, 2, 240, 128), BF), V((2, 8, 240, 128), BF),
            V((4, 2, 128, 128), BF), V((8, 128, 128), BF),
            V((4, 160, 256), BF), V((4, 160, 256), F32),
            V((2, 160, 128), F32), V((160, 128), F32),
            V((2, 256, 256), BF), V((2, 160, 128), BF), V((2, 160, 1024), BF),
            V((4, 80, 512), F32), V((4, 80, 512), F32), V((4, 80, 512), F32),
            V((2, 80, 512), BF), V((2, 80, 512), BF),
            V((Z, 48, 128), BF), V((Z, 48, 128), BF), V((48, 128), F32), V((48, 128), F32),
            dma((6,)), dma((Z,)), dma((Z,)), dma((Z,)), dma((Z,)), dma((Z,)), dma((Z,)), dma((7,)), dma((7,)), dma((7,)), dma((7,)),
            dma((7,)), dma((7,)), dma((24,)), dma((24,)), dma((32,)), dma((32,)), dma((4,)), dma((4,)),
            dma((2,)), dma((2,)), dma((Z,)), dma((Z,)), dma, dma,
        ],
        compiler_params=pltpu.CompilerParams(
            collective_id=0, has_side_effects=True, vmem_limit_bytes=60 * 1024 * 1024
        ),
        cost_estimate=pl.CostEstimate(flops=2 * 10**9, bytes_accessed=4 * 10**6, transcendentals=10**6),
    )(
        examples, references, cotangent, gate_weight.T, up_weight.T, down_weight, pair_ref.T, points,
        jnp.asarray(compact_rows(), BF), jnp.asarray(part_rows(), BF), jnp.asarray(reference_rows(), BF),
        jnp.asarray(pack_rows(), BF), jnp.asarray(row_table()),
    )


def solution(mesh):
    split = Mesh(mesh.devices.reshape(2, Z, 2, 4, 2), ("h", "z", "c", "x", "l"))
    wide, narrow = ("h", "z", "c"), ("x", "l")
    return jax.shard_map(
        on_device,
        mesh=split,
        in_specs=(
            P(wide, narrow), P(wide, narrow), P(narrow, wide), P(narrow, wide),
            P(wide, narrow), P(wide, narrow), P(), P(),
        ),
        out_specs=P(wide, narrow),
        check_vma=False,
    )
```

```python
import functools

import jax
import jax.numpy as jnp
import numpy as np
from jax import lax
from jax.experimental import pallas as pl
from jax.experimental.pallas import tpu as pltpu
from jax.sharding import Mesh
from jax.sharding import PartitionSpec as P

MESH = pl.DeviceIdType.MESH
BF = jnp.bfloat16
F32 = jnp.float32
Z = 16
NT = (((1,), (1,)), ((), ()))


def dot(a, b):
    return jnp.dot(a, b, preferred_element_type=F32)


def dot_nt(a, b):
    return lax.dot_general(a, b, NT, preferred_element_type=F32)


OFFSETS = (0, 1, -1, 2, -2, 4, -4, 8, 3, -3, 5, -5, 6, -6, 7, -7)


def slot_of(offset):
    return next(p for p in range(Z) if (OFFSETS[p] - offset) % Z == 0)


def compact_rows():
    s = np.zeros((96, 128), np.float32)
    for t in range(8):
        for r in range(10):
            s[10 * t + r, 16 * t + r] = 1
        for i in range(2):
            s[80 + 2 * t + i, 16 * t + 10 + i] = 1
    return s


def part_rows():
    s = np.zeros((640, 640), np.float32)
    for t in range(8):
        for q in range(8):
            for i in range(5):
                s[80 * t + 5 * q + i, 80 * q + 10 * t + i] = 1
                s[80 * t + 40 + 5 * q + i, 80 * q + 10 * t + 5 + i] = 1
    return s


def reference_rows():
    s = np.zeros((256, 256), np.float32)
    for t in range(8):
        for q in range(Z):
            for i in range(2):
                s[32 * t + 2 * q + i, 16 * q + 2 * t + i] = 1
    return s


def pack_rows():
    s = np.zeros((384, 320), np.float32)
    for p in range(8):
        for t in range(4):
            for i in range(10):
                s[p * 48 + 10 * t + i, 80 * t + 40 * (i // 5) + 5 * p + i % 5] = 1
    return s


def row_table():
    t = np.zeros((160, 128), np.int32)
    for r in range(160):
        t[r, 0] = OFFSETS[8 * (r // 80) + r % 40 // 5]
        t[r, 1] = 5 * (r % 80 // 40) + r % 5
    return t


def kernel(
    ex_ref, rf_ref, ct_ref, wg_hbm, wu_hbm, wd_hbm, pair_ref, points_ref,
    sel0_ref, perm_hbm, rperm_hbm, pack_hbm, table_ref,
    out_ref,
    wg, wu, wd, perm, rperm, pack, wcat, wd2, xbuf, rbuf, xs, xr, sendb, recvb, sendr, recvr, onehot, base, acce, accu,
    bdiag, sendc, full, d1send, d1recv, keep, d2send, d2recv, d3send, d3recv, fin, finr,
    wsem, zs, zr, ws, wr, ys, yr, hs, hr, ms, mr, gs, gr, bs, br, cs, cr, d1s, d1r, d2s, d2r, d3s, d3r, fs, fr,
):
    h, z, c = lax.axis_index("h"), lax.axis_index("z"), lax.axis_index("c")
    x, l = lax.axis_index("x"), lax.axis_index("l")
    mine = 2 * x + l
    m, mh = 2 * h + c, 2 * (1 - h) + c
    pending = []

    def send(src, dst, ssem, rsem, dev):
        cp = pltpu.make_async_remote_copy(
            src_ref=src, dst_ref=dst, send_sem=ssem, recv_sem=rsem, device_id=dev, device_id_type=MESH
        )
        cp.start()
        pending.append(cp)
        return cp

    def along(offset):
        return {"z": lax.rem(z + offset + Z, Z)}

    facing, mate = {"h": 1 - h}, {"c": 1 - c}
    peers = [{"x": lax.rem(x + i // 2, 4), "l": lax.rem(l + i % 2, 2)} for i in range(8)]
    barrier = pltpu.get_barrier_semaphore()
    for dev in [along(e) for e in (8, 4, -4, 2, -2, 1, -1)] + [facing] + peers[1:] + [mate]:
        pl.semaphore_signal(barrier, inc=1, device_id=dev, device_id_type=MESH)

    loads = [
        pltpu.make_async_copy(a, b, wsem.at[i])
        for i, (a, b) in enumerate(((wg_hbm, wg), (wu_hbm, wu), (wd_hbm, wd), (perm_hbm, perm), (rperm_hbm, rperm), (pack_hbm, pack)))
    ]
    for cp in loads:
        cp.start()

    t = jnp.concatenate(
        [ex_ref[...].astype(F32), ct_ref[...].astype(F32), rf_ref[...].astype(F32), jnp.zeros((4, 1024), F32)], axis=0
    ).astype(BF)
    t = jnp.concatenate([t[:, 128 * i : 128 * i + 128] for i in range(8)], axis=0)
    t = dot(sel0_ref[...], t).astype(BF)
    xbuf[0, m, 0] = t[:80]
    rbuf[m, 0] = t[80:]
    pl.semaphore_wait(barrier, 16)

    def block(p, who):
        return xbuf.at[p // 8, who, p % 8]

    zc, wc, yc = {}, {}, {}

    def zsend(offset, e):
        p = slot_of(offset - e)
        zc[p] = send(block(slot_of(offset), m), block(p, m), zs.at[p], zr.at[p], along(e))

    def ysend(offset, e):
        p = slot_of(offset - e)
        yc[p] = send(block(slot_of(offset), mh), block(p, mh), ys.at[p], yr.at[p], along(e))

    def wsend(offset, e):
        p = slot_of(offset - e)
        wc[p] = send(rbuf.at[m, slot_of(offset)], rbuf.at[m, p], ws.at[p], wr.at[p], along(e))

    for e in (8, 4, -4, 2, -2, 1, -1):
        wsend(0, e)
    for e in (8, 4, -4):
        zsend(0, e)

    for cp in loads:
        cp.wait()

    def prep(a):
        w0 = (0, 0, 128, 256)[a]
        kk = min(256, 448 - w0)
        k = lax.broadcasted_iota(jnp.int32, (256, kk), 1) + w0
        n = lax.broadcasted_iota(jnp.int32, (256, kk), 0)
        r = n & 127
        first = 56 * (2 * a + (n >> 7))
        gate = (r < 56) & (k == first + r)
        up = (r >= 64) & (r < 120) & (k == first + r - 64)
        sg = jnp.where(gate, 1.0, 0.0).astype(BF)
        su = jnp.where(up, 1.0, 0.0).astype(BF)
        sd = jnp.where(gate | up, 1.0, 0.0).astype(BF)
        for b in range(4):
            cols = pl.ds(256 * b, 256)
            rows = pl.ds(w0, kk)
            wcat[pl.ds(256 * a, 256), cols] = (dot(sg, wg[rows, cols]) + dot(su, wu[rows, cols])).astype(BF)
            wd2[pl.ds(256 * a, 256), cols] = dot(sd, wd[rows, cols]).astype(BF)

    hc, mc, gc = {}, {}, {}

    groups = ((0, 1), (1, 5), (5, 8), (8, 12), (12, 16), (0, 8), (8, 16))

    def group(k, who):
        first, last = groups[k]
        if k > 4:
            return rbuf.at[who, pl.ds(first, last - first)]
        return xbuf.at[first // 8, who, pl.ds(first % 8, last - first)]

    def spread(k):
        for p in range(*groups[k]):
            if p not in (0, 5, 6, 7):
                (wc if k > 4 else zc)[p].wait_recv()
        at = group(k, m)
        if k not in (3, 4):
            hc[k] = send(at, at, hs.at[k], hr.at[k], facing)
        mc[k] = send(at, at, ms.at[k], mr.at[k], mate)

    def onward(k):
        if k in (3, 4):
            for p in range(*groups[k]):
                yc[p].wait_recv()
        else:
            hc[k].wait_recv()
        at = group(k, mh)
        gc[k] = send(at, at, gs.at[k], gr.at[k], mate)

    def to_owners(src, dst, at):
        for i in (7, 5, 3, 4, 1, 6, 2):
            n = 8 * at + i
            to = src.at[lax.rem(x + i // 2, 4), lax.rem(l + i % 2, 2)]
            bc[at, i] = send(to, dst.at[i], bs.at[n], br.at[n], peers[i])

    def reference_work():
        for g in (5, 6):
            mc[g].wait_recv()
            gc[g].wait_recv()
        for i in range(4):
            o = dot(rperm[...], rbuf[i].reshape(256, 128)).astype(BF)
            for t in range(8):
                xr[32 * i : 32 * i + 32, 128 * t : 128 * t + 128] = o[32 * t : 32 * t + 32]

        @pl.loop(0, 4)
        def _(n):
            cols = pl.ds(pl.multiple_of(256 * n, 256), 256)
            p = dot_nt(xr[...], wcat[cols, :]).astype(BF)
            for e in range(2):
                sendr[n, e] = p[:, 128 * e : 128 * e + 128]

        to_owners(sendr, recvr, 2)

    def work(k):
        for g in ((0, 1, 2), (3, 4))[k]:
            mc[g].wait_recv()
            gc[g].wait_recv()
        for i in range(2):
            o = [dot(perm[...], xbuf[k, 2 * i + j].reshape(640, 128)) for j in range(2)]
            for t in range(8):
                for b in range(2):
                    rows = slice(80 * t + 40 * b, 80 * t + 40 * b + 40)
                    at = slice(160 * b + 80 * i, 160 * b + 80 * i + 80)
                    xs[at, 128 * t : 128 * t + 128] = jnp.concatenate([o[0][rows], o[1][rows]], axis=0).astype(BF)
        left = lax.broadcasted_iota(jnp.int32, (80, 256), 1) & 127

        @pl.loop(0, 4)
        def _(n):
            cols = pl.ds(pl.multiple_of(256 * n, 256), 256)
            p = dot_nt(xs[0:160], wcat[cols, :]).astype(BF)
            d = dot_nt(xs[160:320], wd2[cols, :])
            d = jnp.where(left < 64, d[:80], d[80:]).astype(BF)
            for e in range(2):
                sendb[k, n, e, 0:160] = p[:, 128 * e : 128 * e + 128]
                sendb[k, n, e, 160:240] = d[:, 128 * e : 128 * e + 128]

        to_owners(sendb.at[k], recvb.at[k], k)

    bc = {}

    def owner_sum(k):
        total = sendb[k, x, l].astype(F32)
        for i in range(1, 8):
            bc[k, i].wait_recv()
            total = total + recvb[k, i].astype(F32)
        e0, e1 = total[0:80], total[80:160]
        half = lax.broadcasted_iota(jnp.int32, (80, 128), 1) < 64
        acce[0, 80 * k : 80 * k + 80] = jnp.where(half, e0, pltpu.roll(e1, 64, 1))
        acce[1, 80 * k : 80 * k + 80] = jnp.where(half, pltpu.roll(e0, 64, 1), e1)
        accu[80 * k : 80 * k + 80] = total[160:240]

    def choose():
        off, place = table_ref[:, 0:1], table_ref[:, 1:2]
        want = ((z + off + Z) & (Z - 1)) * 10 + place
        turn = jnp.where(lax.broadcasted_iota(jnp.int32, (160, 160), 1) == want, 1.0, 0.0).astype(BF)
        for hh in range(2):
            picks = pair_ref[...].astype(F32)[:, 160 * hh : 160 * hh + 160].astype(BF)
            r = dot_nt(turn, picks).astype(jnp.int32)
            delta = (((r >> 2) & 15) - z + Z) & (Z - 1)
            slot = jnp.zeros_like(delta)
            for p in range(1, Z):
                slot = jnp.where(delta == OFFSETS[p] % Z, p, slot)
            pos = (r >> 6) * 64 + ((r >> 1) & 1) * 32 + slot * 2 + (r & 1)
            lane = lax.broadcasted_iota(jnp.int32, (160, 128), 1)
            for p in range(4):
                onehot[p, :, 128 * hh : 128 * hh + 128] = jnp.where(lane == pos[:, p : p + 1], 1.0, 0.0).astype(BF)

    spread(0)
    for i in range(4):
        prep(i)
    for e in (2, -2, 1, -1):
        zsend(0, e)
    def near(far, to):
        for offset, e in {
            7: ((8, 1), (8, -1)), 5: ((4, -2), (4, 1), (4, -1)), 6: ((-4, 2), (-4, 1), (-4, -1))
        }[far]:
            to(offset, e)

    for got, to in ((wc, wsend), (zc, zsend)):
        for p in (7, 5, 6):
            got[p].wait_recv()
            near(p, to)
    spread(2)
    spread(5)
    choose()
    onward(2)
    for p in (7, 5, 6):
        near(p, ysend)
    spread(1)
    spread(6)
    onward(0)
    onward(5)
    onward(6)
    reference_work()
    onward(1)
    spread(3)
    spread(4)
    work(0)
    onward(3)
    onward(4)
    work(1)

    def bases():
        refs = sendr[x, l].astype(F32)
        for i in range(1, 8):
            bc[2, i].wait_recv()
            refs = refs + recvr[i].astype(F32)
        turned = pltpu.roll(refs, 64, 1)
        left = lax.broadcasted_iota(jnp.int32, (128, 128), 1) < 64
        diag = (
            jnp.where(left, refs, 0.0), jnp.where(left, 0.0, turned),
            jnp.where(left, turned, 0.0), jnp.where(left, 0.0, refs),
        )
        for n, block in enumerate(diag):
            high = block.astype(BF)
            low = (block - high.astype(F32)).astype(BF)
            at = (slice(128 * (n % 2), 128 * (n % 2) + 128), slice(128 * (n // 2), 128 * (n // 2) + 128))
            bdiag[(0, *at)] = high
            bdiag[(1, *at)] = low
        for p in range(4):
            base[p] = dot(onehot[p], bdiag[0]) + dot(onehot[p], bdiag[1])

    bases()
    owner_sum(0)

    alphas = [points_ref[i].astype(F32) * 0.125 for i in range(8)]

    lanes = pl.ds(pl.multiple_of(128 * mine, 128), 128)
    cc = {}

    def coefs(part):
        @pl.loop(0, 5)
        def _(n):
            rows = pl.ds(pl.multiple_of(80 * part + 16 * n, 16), 16)
            eg, eu, up = acce[0, rows], acce[1, rows], accu[rows]
            cg = jnp.zeros((16, 128), F32)
            cu = jnp.zeros((16, 128), F32)
            for p in range(4):
                bg, bu = base[p, rows, 0:128], base[p, rows, 128:256]
                dg, du = eg - bg, eu - bu
                for a in alphas:
                    g = bg + a * dg
                    u = bu + a * du
                    s = 0.5 * jnp.tanh(0.5 * g) + 0.5
                    gs = g * s
                    cu = cu + gs
                    cg = cg + u * (s + gs * (1.0 - s))
            cg = up * (cg * (1.0 / 32.0))
            cu = up * (cu * (1.0 / 32.0))
            half = lax.broadcasted_iota(jnp.int32, (16, 128), 1) < 64
            first = pl.ds(pl.multiple_of(16 * n, 16), 16)
            second = pl.ds(pl.multiple_of(80 + 16 * n, 16), 16)
            sendc[part, first, :] = jnp.where(half, cg, pltpu.roll(cu, 64, 1)).astype(BF)
            sendc[part, second, :] = jnp.where(half, pltpu.roll(cg, 64, 1), cu).astype(BF)

        for b, hh in enumerate((1 - h, h)):
            rows = pl.ds(pl.multiple_of(80 * hh, 16), 80)
            for i in range(1, 8):
                n = 16 * part + 8 * b + i
                cc[part, b, i] = send(
                    sendc.at[part, rows], full.at[part, rows, lanes], cs.at[n], cr.at[n], peers[i]
                )
        full[part, :, lanes] = sendc[part]

    def product(part, hh, col, into, at):
        rows = pl.ds(pl.multiple_of(80 * hh, 16), 80)

        @pl.loop(0, 2)
        def _(n):
            w = pl.ds(pl.multiple_of(512 * col + 256 * n, 256), 256)
            into[at, :, pl.ds(pl.multiple_of(256 * n, 256), 256)] = dot(full[part, rows, :], wcat[:, w])

    d1, d2, d3 = {}, {}, {}

    def products(part):
        for i in range(1, 8):
            cc[part, 0, i].wait_recv()
        at = 2 * part

        def lend(i, hh):
            product(part, hh, 1 - c, d1send, at + i)
            d1[at + i] = send(d1send.at[at + i], d1recv.at[at + i], d1s.at[at + i], d1r.at[at + i], mate)

        lend(0, 1 - h)
        product(part, 1 - h, c, keep, at)
        d1[at].wait_recv()
        d2send[part] = (keep[at] + d1recv[at]).astype(BF)
        d2[part] = send(d2send.at[part], d2recv.at[part], d2s.at[part], d2r.at[part], facing)
        for i in range(1, 8):
            cc[part, 1, i].wait_recv()
        lend(1, h)
        product(part, h, c, keep, at + 1)

    def scatter(part):
        d1[2 * part + 1].wait_recv()
        v = keep[2 * part + 1] + d1recv[2 * part + 1]
        d2[part].wait_recv()
        v = (v + d2recv[part].astype(F32)).astype(BF)
        v = jnp.concatenate([v[:, 128 * t : 128 * t + 128] for t in range(4)], axis=0)
        d3send[8 * part : 8 * part + 8] = dot(pack[...], v).astype(BF).reshape(8, 48, 128)
        for p in range(8 * part, 8 * part + 8):
            if p:
                d3[p] = send(d3send.at[p], d3recv.at[p], d3s.at[p], d3r.at[p], along(OFFSETS[p]))

    coefs(0)
    owner_sum(1)
    coefs(1)
    products(0)
    scatter(0)
    products(1)
    scatter(1)
    total = d3send[0].astype(F32)
    for p in range(1, Z):
        d3[p].wait_recv()
        total = total + d3recv[p].astype(F32)
    fin[...] = total
    last = send(fin, finr, fs, fr, mate)
    last.wait_recv()
    other = finr[...]
    first = c == 0
    parts = []
    for block in (jnp.where(first, total, other), jnp.where(first, other, total)):
        for t in range(4):
            parts.append(jnp.where(first, block[10 * t : 10 * t + 5], block[10 * t + 5 : 10 * t + 10]))
    out_ref[...] = jnp.concatenate(parts, axis=1).astype(BF)
    for cp in pending:
        cp.wait_send()


def on_device(examples, references, gate_weight, up_weight, down_weight, cotangent, pair_ref, points):
    vm = pl.BlockSpec(memory_space=pltpu.VMEM)
    hbm = pl.BlockSpec(memory_space=pltpu.HBM)
    sm = pl.BlockSpec(memory_space=pltpu.SMEM)
    dma = pltpu.SemaphoreType.DMA
    V = pltpu.VMEM
    return pl.pallas_call(
        kernel,
        out_shape=jax.ShapeDtypeStruct((5, 1024), BF),
        in_specs=[vm, vm, vm, hbm, hbm, hbm, vm, sm, vm, hbm, hbm, hbm, vm],
        out_specs=vm,
        scratch_shapes=[
            V((448, 1024), BF), V((448, 1024), BF), V((448, 1024), BF),
            V((640, 640), BF), V((256, 256), BF), V((384, 320), BF),
            V((1024, 1024), BF), V((1024, 1024), BF),
            V((2, 4, 8, 80, 128), BF), V((4, Z, 16, 128), BF), V((320, 1024), BF), V((128, 1024), BF),
            V((2, 4, 2, 240, 128), BF), V((2, 8, 240, 128), BF),
            V((4, 2, 128, 128), BF), V((8, 128, 128), BF),
            V((4, 160, 256), BF), V((4, 160, 256), F32),
            V((2, 160, 128), F32), V((160, 128), F32),
            V((2, 256, 256), BF), V((2, 160, 128), BF), V((2, 160, 1024), BF),
            V((4, 80, 512), F32), V((4, 80, 512), F32), V((4, 80, 512), F32),
            V((2, 80, 512), BF), V((2, 80, 512), BF),
            V((Z, 48, 128), BF), V((Z, 48, 128), BF), V((48, 128), F32), V((48, 128), F32),
            dma((6,)), dma((Z,)), dma((Z,)), dma((Z,)), dma((Z,)), dma((Z,)), dma((Z,)), dma((7,)), dma((7,)), dma((7,)), dma((7,)),
            dma((7,)), dma((7,)), dma((24,)), dma((24,)), dma((32,)), dma((32,)), dma((4,)), dma((4,)),
            dma((2,)), dma((2,)), dma((Z,)), dma((Z,)), dma, dma,
        ],
        compiler_params=pltpu.CompilerParams(
            collective_id=0, has_side_effects=True, vmem_limit_bytes=60 * 1024 * 1024
        ),
        cost_estimate=pl.CostEstimate(flops=2 * 10**9, bytes_accessed=4 * 10**6, transcendentals=10**6),
    )(
        examples, references, cotangent, gate_weight.T, up_weight.T, down_weight, pair_ref.T, points,
        jnp.asarray(compact_rows(), BF), jnp.asarray(part_rows(), BF), jnp.asarray(reference_rows(), BF),
        jnp.asarray(pack_rows(), BF), jnp.asarray(row_table()),
    )


def solution(mesh):
    split = Mesh(mesh.devices.reshape(2, Z, 2, 4, 2), ("h", "z", "c", "x", "l"))
    wide, narrow = ("h", "z", "c"), ("x", "l")
    return jax.shard_map(
        on_device,
        mesh=split,
        in_specs=(
            P(wide, narrow), P(wide, narrow), P(narrow, wide), P(narrow, wide),
            P(wide, narrow), P(wide, narrow), P(), P(),
        ),
        out_specs=P(wide, narrow),
        check_vma=False,
    )
```
